512 devices in a mesh: gx: 32 (over x, y), gy: 16 (over z, core).
Axes of the slice: x: 4, y: 8, z: 8, core: 2. Of those that a mesh axis runs over, the one named last changes fastest.
Arguments:
- positions: float32 [3, 1048576], P(None, ('gx', 'gy')), may hold values from 0 to 32, as said below
- density: float32 [1048576], P(('gx', 'gy')), may hold values from 0.5 to 4
- momentum: float32 [3, 1048576], P(None, ('gx', 'gy')), may hold values from -3 to 3
- field: float32 [3, 1048576], P(None, ('gx', 'gy')), may hold values from -3 to 3
- psi: float32 [1048576], P(('gx', 'gy')), may hold values from -3 to 3
- ohmic: float32 [1048576], P(('gx', 'gy')), may hold values from 0.05 to 20
- ambipolar: float32 [1048576], P(('gx', 'gy')), may hold values from 0.02 to 0.3
- ghost_index: int32 [557056], P(('gx', 'gy')), may hold values from 0 to 2047, as said below
- tile_i: int32 [32768], P(('gx', 'gy')), may hold values from 0 to 15, as said below
- tile_j: int32 [32768], P(('gx', 'gy')), may hold values from 0 to 24, as said below
- tile_count: int32 [512], P(('gx', 'gy')), may hold values from 16 to 64, as said below
Outputs:
- density_new: float32 [1048576], P(('gx', 'gy'))
- momentum_new: float32 [3, 1048576], P(None, ('gx', 'gy'))
- field_new: float32 [3, 1048576], P(None, ('gx', 'gy'))
- psi_new: float32 [1048576], P(('gx', 'gy'))
The draws below stay inside these ranges and needn't reach their ends.
Inputs may be any that keep to these rules, and one draw needn't show every extreme that they name: `positions`: x lies in [ix, ix+1) and y in [iy, iy+1) for the owner (ix, iy); z lies in [0, 0.5). `ghost_index`: within one device the 1088 numbers are distinct. `tile_i`: a block of 128 local particles. `tile_j`: a block of 128 in the extended set; the pairs (tile_i, tile_j) of one device are distinct. `tile_count`: the devices of a dense region of three by three slabs use all 64 entries.
All inputs are finite; a program needn't handle non-finite values.
Results may differ from the reference program's by a relative error of at most 0.0003.
Values sent between devices are 32-bit elements; how exact they have to be, the bound alone decides.
A program may use at most 64 MiB of HBM per device.

```python
import math
import jax
import jax.numpy as jnp
from jax import lax

PART_DEV = 2048
TILE = 128
SECTIONS = 4
GHOST_X = 320
GHOST_Y = 160
GHOST_C = 32
GSEND = 1088
EXT_BLOCKS = 25
TILE_MAX = 64
PARTICLES = 1048576
N_GX = 32
N_GY = 16
DEVICES = 512


def ghost_plan(key):
    keys = jax.random.split(jax.random.fold_in(key, 7), DEVICES)
    return jax.vmap(lambda k: jax.random.permutation(k, PART_DEV))(keys).astype(jnp.int32)


def draw_ghost_index(key, part):
    perms = ghost_plan(key)
    return perms[:, :GSEND].reshape(-1).astype(jnp.int32)


def draw_positions(key, part):
    perms = ghost_plan(key)
    rank = jnp.argsort(perms, axis=1).astype(jnp.int32)
    sizes = [GHOST_C, GHOST_X, GHOST_C, GHOST_Y, GHOST_Y, GHOST_C, GHOST_X, GHOST_C]
    bounds = []
    total = 0
    for value in sizes:
        total = total + value
        bounds.append(total)
    which = jnp.zeros(rank.shape, jnp.int32)
    for k in range(7):
        which = which + (rank >= bounds[k]).astype(jnp.int32)
    inside = rank < GSEND
    table_x = jnp.array([-1, -1, -1, 0, 0, 1, 1, 1], jnp.int32)
    table_y = jnp.array([-1, 0, 1, -1, 1, -1, 0, 1], jnp.int32)
    side_x = jnp.where(inside, table_x[which], 0)
    side_y = jnp.where(inside, table_y[which], 0)
    unit = jax.random.uniform(jax.random.fold_in(key, 5), (3, DEVICES, PART_DEV), jnp.float32)

    def placed(value, side):
        return jnp.where(side < 0, 0.25 * value, jnp.where(side > 0, 0.75 + 0.25 * value, value))
    dev = jnp.arange(DEVICES, dtype=jnp.int32)[:, None]
    col_x = (dev // N_GY).astype(jnp.float32)
    col_y = (dev % N_GY).astype(jnp.float32)
    coord_x = col_x + placed(unit[0], side_x)
    coord_y = col_y + placed(unit[1], side_y)
    coord_z = 0.5 * unit[2]
    return jnp.stack([coord_x, coord_y, coord_z]).reshape(3, PARTICLES).astype(jnp.float32)


def tile_lists(key):
    ext_blocks = EXT_BLOCKS
    total = PART_DEV // TILE * ext_blocks
    scores = jax.random.randint(jax.random.fold_in(key, 11), (DEVICES, total), 0, 65536, dtype=jnp.int32)
    scores = scores * total + jnp.arange(total, dtype=jnp.int32)[None, :]
    order = jnp.argsort(scores, axis=1)[:, :TILE_MAX].astype(jnp.int32)
    return ((order // ext_blocks).reshape(-1), (order % ext_blocks).reshape(-1))


def draw_tile_i(key, part):
    return tile_lists(key)[0].astype(jnp.int32)


def draw_tile_j(key, part):
    return tile_lists(key)[1].astype(jnp.int32)


def draw_tile_count(key, part):
    centre_x = jax.random.randint(jax.random.fold_in(key, 23), (), 0, N_GX, dtype=jnp.int32)
    centre_y = jax.random.randint(jax.random.fold_in(key, 29), (), 0, N_GY, dtype=jnp.int32)
    dev = jnp.arange(DEVICES, dtype=jnp.int32)
    core = (jnp.abs(dev // N_GY - centre_x) <= 1) & (jnp.abs(dev % N_GY - centre_y) <= 1)
    lowest = max(1, TILE_MAX // 4)
    far_dev = (centre_x + N_GX // 2) % N_GX * N_GY + (centre_y + N_GY // 2) % N_GY
    base = jax.random.randint(jax.random.fold_in(key, 31), (DEVICES,), lowest, max(lowest, TILE_MAX // 2) + 1, dtype=jnp.int32)
    base = jnp.where(dev == far_dev, lowest, base)
    return jnp.where(core, TILE_MAX, base).astype(jnp.int32)


def levels(key, extent, shards, low, top_value):
    loudness = 1.0
    for axis_at, parts in shards:
        steps = jax.random.uniform(jax.random.fold_in(jax.random.fold_in(key, 6), axis_at), (parts,), jnp.float32, low / len(shards), top_value / len(shards))
        loudness = loudness * jnp.repeat(jnp.exp(steps), extent[axis_at] // parts).reshape((-1,) + (1,) * (len(extent) - 1 - axis_at))
    return loudness


def gaussian(key, shape, width, bound, shards=(), held_as=jnp.bfloat16):
    level = levels(key, shape, shards, -0.22, 0.18) if shards else 1.0
    entries = jax.random.normal(key, shape, jnp.float32) * width * level
    return jnp.minimum(jnp.maximum(entries, -bound), bound).astype(held_as)


def setup_inputs(seed: int = 0) -> dict:
    streams_of = jax.random.split(jax.random.key(seed), 12)
    positions = draw_positions(jax.random.fold_in(streams_of[11], 71), 0)
    density = jnp.clip(jnp.exp(math.log(4.0) - 2.0794415 * jax.random.uniform(streams_of[1], (PARTICLES,), jnp.float32) ** levels(streams_of[1], (PARTICLES,), ((0, 512),), -0.2, 0.2)), 0.5, 4.0)
    momentum = gaussian(streams_of[2], (3, PARTICLES), 0.5, 3.0, ((1, 512),), jnp.float32)
    field = gaussian(streams_of[3], (3, PARTICLES), 0.5, 3.0, ((1, 512),), jnp.float32)
    psi = gaussian(streams_of[4], (PARTICLES,), 0.5, 3.0, ((0, 512),), jnp.float32)
    ohmic = jnp.clip(jnp.exp(math.log(20.0) - 5.9914645 * jax.random.uniform(streams_of[5], (PARTICLES,), jnp.float32) ** levels(streams_of[5], (PARTICLES,), ((0, 512),), -0.2, 0.2)), 0.05, 20.0)
    ambipolar = jnp.clip(jnp.exp(math.log(0.3) - 2.7080503 * jax.random.uniform(streams_of[6], (PARTICLES,), jnp.float32) ** levels(streams_of[6], (PARTICLES,), ((0, 512),), -0.2, 0.2)), 0.02, 0.3)
    ghost_index = draw_ghost_index(jax.random.fold_in(streams_of[11], 71), 0)
    tile_i = draw_tile_i(jax.random.fold_in(streams_of[11], 71), 0)
    tile_j = draw_tile_j(jax.random.fold_in(streams_of[11], 71), 0)
    tile_count = draw_tile_count(jax.random.fold_in(streams_of[11], 71), 0)
    return {"positions": positions, "density": density, "momentum": momentum, "field": field, "psi": psi, "ohmic": ohmic, "ambipolar": ambipolar, "ghost_index": ghost_index, "tile_i": tile_i, "tile_j": tile_j, "tile_count": tile_count}


DIRECTIONS = [(-1, -1), (-1, 0), (-1, 1), (0, -1), (0, 1), (1, -1), (1, 0), (1, 1)]
courant = 0.3
damping = 0.5

def ghost_sizes():
    return [GHOST_C, GHOST_X, GHOST_C, GHOST_Y, GHOST_Y, GHOST_C, GHOST_X, GHOST_C]

def ghost_offsets():
    sizes = ghost_sizes()
    starts = [0]
    for value in sizes[:-1]:
        starts.append(starts[-1] + value)
    return starts

def rkl_table(sections):
    wfirst = 4.0 / (sections * sections + sections - 2)
    bvals = [1.0 / 3.0, 1.0 / 3.0, 1.0 / 3.0] + [(j * j + j - 2) / (2.0 * j * (j + 1)) for j in range(3, sections + 1)]
    first = bvals[1] * wfirst
    rows = []
    for j in range(2, sections + 1):
        mu_j = (2.0 * j - 1.0) / j * bvals[j] / bvals[j - 1]
        nu_j = -(j - 1.0) / j * bvals[j] / bvals[j - 2]
        mut_j = mu_j * wfirst
        rows.append((mu_j, nu_j, mut_j, -(1.0 - bvals[j - 1]) * mut_j))
    return (first, rows)

def kernel_tile(near, far):
    dist = (near[0][..., :, None] - far[0][..., None, :]) ** 2
    dist = dist + (near[1][..., :, None] - far[1][..., None, :]) ** 2
    dist = dist + (near[2][..., :, None] - far[2][..., None, :]) ** 2
    base = jnp.maximum(1.0 - 4.0 * dist, 0.0)
    return base * base

def flux_rows(ext, ch):
    posit = ext[0:3]
    live = ext[3]
    rho = ext[4]
    vel = ext[5:8]
    bfl = ext[8:11]
    cpsi = ext[11]
    speed = ext[12]
    mom = rho * vel
    ptot = rho + 0.5 * lax.optimization_barrier(jnp.sum(bfl * bfl, axis=0))
    fluxes = []
    for d in range(3):
        rows_d = [mom[d]]
        for k in range(3):
            term = mom[k] * vel[d] - bfl[k] * bfl[d]
            rows_d.append(term + ptot if k == d else term)
        for k in range(3):
            term = vel[d] * bfl[k] - bfl[d] * vel[k]
            rows_d.append(term + cpsi if k == d else term)
        rows_d.append(ch * ch * bfl[d])
        fluxes.append(jnp.stack(rows_d))
    flux = jnp.stack(fluxes)
    state = jnp.concatenate([rho[None], mom, bfl, cpsi[None]], axis=0)
    gsum = posit[0] * flux[0] + posit[1] * flux[1] + posit[2] * flux[2]
    return jnp.concatenate([live[None], posit, flux.reshape(24, -1), gsum, speed * state, speed[None], state], axis=0)

def add_tile(acc, weight, qblock, start):
    part = lax.dot_general(qblock, weight, (((1,), (1,)), ((), ())), precision=lax.Precision.HIGHEST, preferred_element_type=jnp.float32)
    cur = lax.dynamic_slice_in_dim(acc, start, TILE, 1)
    return lax.dynamic_update_slice_in_dim(acc, cur + part, start, 1)

def accumulate(qext, pos_ext, tiles_i, tiles_j, count, nlocal):

    def step(t, acc):
        start_i = (tiles_i[t] * TILE).astype(jnp.int32)
        start_j = (tiles_j[t] * TILE).astype(jnp.int32)
        near = lax.dynamic_slice_in_dim(pos_ext, start_i, TILE, 1)
        far = lax.dynamic_slice_in_dim(pos_ext, start_j, TILE, 1)
        weight = kernel_tile(near, far)
        qblock = lax.dynamic_slice_in_dim(qext, start_j, TILE, 1)
        return add_tile(acc, weight, qblock, start_i)
    acc = jnp.zeros((qext.shape[0], nlocal), jnp.float32)
    return lax.fori_loop(0, count, step, acc)

def hydro_rate(acc, local):
    count_n = acc[0]
    num = acc.shape[1]
    wflux = acc[4:28].reshape(3, 8, num)
    flux = local[4:28].reshape(3, 8, num)
    posit = local[1:4]
    speed = local[44]
    state = local[45:53]
    central = acc[28:36]
    for d in range(3):
        central = central + flux[d] * (acc[1 + d] - posit[d] * count_n) - posit[d] * wflux[d]
    dissip = speed * (acc[45:53] - state * count_n) + acc[36:44] - state * acc[44]
    return ((0.5 * dissip - 0.5 * central) / (1.0 + count_n), count_n)

def diffusion_rate(acc, bloc, etaloc, count_n):
    return 0.5 * (etaloc * (acc[0:3] - bloc * count_n) + acc[3:6] - bloc * acc[6]) / (1.0 + count_n)

def reference(positions, density, momentum, field, psi, ohmic, ambipolar, ghost_index, tile_i, tile_j, tile_count):
    ndev = N_GX * N_GY
    sizes = ghost_sizes()
    starts = ghost_offsets()

    def per_dev(rows):
        return rows.reshape(rows.shape[0], ndev, PART_DEV).transpose(1, 0, 2)

    def to_global(rows):
        return rows.transpose(1, 0, 2).reshape(rows.shape[1], ndev * PART_DEV)
    gidx = ghost_index.reshape(N_GX, N_GY, GSEND)

    def assemble(dev_rows):
        nrow = dev_rows.shape[1]
        grid = dev_rows.reshape(N_GX, N_GY, nrow, PART_DEV)
        pieces = []
        for p, q in DIRECTIONS:
            dsend = DIRECTIONS.index((-p, -q))
            segment = gidx[:, :, starts[dsend]:starts[dsend] + sizes[dsend]]
            idx = jnp.broadcast_to(segment[:, :, None, :], (N_GX, N_GY, nrow, sizes[dsend]))
            sent = jnp.take_along_axis(grid, idx, axis=3)
            padded = jnp.pad(sent, ((1, 1), (1, 1), (0, 0), (0, 0)))
            pieces.append(padded[1 + p:1 + p + N_GX, 1 + q:1 + q + N_GY])
        ghosts = jnp.concatenate(pieces, axis=3).reshape(ndev, nrow, GSEND)
        filler = jnp.zeros((ndev, nrow, EXT_BLOCKS * TILE - PART_DEV - GSEND), jnp.float32)
        return jnp.concatenate([dev_rows, ghosts, filler], axis=2)
    velocity = momentum / density
    speed = jnp.sqrt(1.0 + lax.optimization_barrier(jnp.sum(field * field, axis=0)) / density)
    ch = jnp.max(speed)
    dt = courant / ch
    fac = ambipolar / (density * jnp.sqrt(density))
    live = jnp.ones_like(density)
    payload = jnp.concatenate([positions, live[None], density[None], velocity, field, psi[None], speed[None], ohmic[None], fac[None]], axis=0)
    ext = assemble(per_dev(payload))
    tiles_i = tile_i.reshape(ndev, TILE_MAX)
    tiles_j = tile_j.reshape(ndev, TILE_MAX)

    def hydro_one(args):
        ext_d, ti_d, tj_d, cnt = args
        qext = flux_rows(ext_d, ch)
        acc = accumulate(qext, ext_d[0:3], ti_d, tj_d, cnt, PART_DEV)
        return hydro_rate(acc, qext[:, :PART_DEV])
    rates, counts = lax.map(hydro_one, (ext, tiles_i, tiles_j, tile_count))
    rate = to_global(rates)
    count_n = counts.reshape(ndev * PART_DEV)
    density_new = density + dt * rate[0]
    momentum_new = momentum + dt * rate[1:4]
    yzero = field + dt * rate[4:7]
    psi_new = (psi + dt * rate[7]) * jnp.exp(-damping * dt * ch)
    pos_ext = ext[:, 0:3]

    def operator(bfl):
        eta = ohmic + fac * lax.optimization_barrier(jnp.sum(bfl * bfl, axis=0))
        ext2 = assemble(per_dev(jnp.concatenate([bfl, eta[None]], axis=0)))

        def one(args):
            e2, pe, ti_d, tj_d, cnt = args
            qext = jnp.concatenate([e2[0:3], e2[3][None] * e2[0:3], e2[3][None]], axis=0)
            return accumulate(qext, pe, ti_d, tj_d, cnt, PART_DEV)
        acc = to_global(lax.map(one, (ext2, pos_ext, tiles_i, tiles_j, tile_count)))
        return diffusion_rate(acc, bfl, eta, count_n)
    first, rows = rkl_table(SECTIONS)
    lzero = operator(yzero)
    older = yzero
    prev = yzero + first * dt * lzero
    for mu_j, nu_j, mut_j, gam_j in rows:
        nxt = mu_j * prev + nu_j * older + (1.0 - mu_j - nu_j) * yzero + mut_j * dt * operator(prev) + gam_j * dt * lzero
        older = prev
        prev = nxt
    return (density_new, momentum_new, prev, psi_new)
```

```python
import jax
import jax.numpy as jnp
from jax import lax
from jax.experimental import pallas as pl
from jax.experimental.pallas import tpu as pltpu
from jax.sharding import PartitionSpec as P

TILE = 128
SECTIONS = 4
SIZES = [32, 320, 32, 160, 160, 32, 320, 32]
DIRECTIONS = [(-1, -1), (-1, 0), (-1, 1), (0, -1), (0, 1), (1, -1), (1, 0), (1, 1)]
STARTS = [sum(SIZES[:d]) for d in range(8)]
BLOCKS = 16
GBLOCKS = 9
TILES = 64
COURANT = 0.3
DAMPING = 0.5
MESH = pl.DeviceIdType.MESH
F32 = jnp.float32
BF16 = jnp.bfloat16

PIECES = []
OFFSET = []
for d in range(8):
    OFFSET.append(len(PIECES))
    for k in range(STARTS[d] // TILE, (STARTS[d] + SIZES[d] - 1) // TILE + 1):
        lo = max(STARTS[d] - k * TILE, 0)
        hi = min(STARTS[d] + SIZES[d] - k * TILE, TILE)
        PIECES.append((d, k, lo, hi))
COUNT = [sum(1 for p in PIECES if p[0] == d) for d in range(8)]
NPIECE = len(PIECES)

QROWS = 40


def rkl_table(sections):
    wfirst = 4.0 / (sections * sections + sections - 2)
    bvals = [1.0 / 3.0] * 3 + [(j * j + j - 2) / (2.0 * j * (j + 1)) for j in range(3, sections + 1)]
    rows = [(1.0, 0.0, 0.0, bvals[1] * wfirst, 0.0)]
    for j in range(2, sections + 1):
        mu = (2.0 * j - 1.0) / j * bvals[j] / bvals[j - 1]
        nu = -(j - 1.0) / j * bvals[j] / bvals[j - 2]
        mut = mu * wfirst
        rows.append((mu, nu, 1.0 - mu - nu, mut, -(1.0 - bvals[j - 1]) * mut))
    return rows


def q_rows(x, live, rho, mom, bfl, psi, speed):
    inv = 1.0 / rho
    vel = [m * inv for m in mom]
    ptot = rho + 0.5 * (bfl[0] * bfl[0] + bfl[1] * bfl[1] + bfl[2] * bfl[2])
    state = [rho, *mom, *bfl, psi]
    t = {}
    for a in range(3):
        for b in range(a, 3):
            v = mom[b] * vel[a] - bfl[b] * bfl[a]
            t[a, b] = t[b, a] = v + ptot if a == b else v
    ind = {}
    for a in range(3):
        for b in range(a + 1, 3):
            ind[a, b] = vel[a] * bfl[b] - bfl[a] * vel[b]
    gsum = [x[0] * mom[0] + x[1] * mom[1] + x[2] * mom[2]]
    for k in range(3):
        gsum.append(x[0] * t[0, k] + x[1] * t[1, k] + x[2] * t[2, k])
    gsum.append(x[0] * psi - x[1] * ind[0, 1] - x[2] * ind[0, 2])
    gsum.append(x[0] * ind[0, 1] + x[1] * psi - x[2] * ind[1, 2])
    gsum.append(x[0] * ind[0, 2] + x[1] * ind[1, 2] + x[2] * psi)
    gsum.append(x[0] * bfl[0] + x[1] * bfl[1] + x[2] * bfl[2])
    return [
        live, *x, *state, *[speed * u for u in state], speed,
        t[0, 0], t[0, 1], t[0, 2], t[1, 1], t[1, 2], t[2, 2],
        ind[0, 1], ind[0, 2], ind[1, 2], *gsum,
    ]


def flux_of(q):
    m, b, psi = q[5:8], q[8:11], q[11]
    t = {(0, 0): q[21], (0, 1): q[22], (0, 2): q[23], (1, 1): q[24], (1, 2): q[25], (2, 2): q[26]}
    i01, i02, i12 = q[27:30]
    ind = [[psi, i01, i02], [-i01, psi, i12], [-i02, -i12, psi]]
    return [[m[d], *[t[min(d, k), max(d, k)] for k in range(3)], *ind[d], b[d]] for d in range(3)]


def kernel(
    tab, pos, rho_r, mom_r, bfl_r, psi_r, ohm_r, amb_r, gi_r,
    rho_o, mom_o, bfl_o, psi_o,
    pk, lane_b, blk_b, pay, paysend, payrecv, ghp, qp, qt, qb, xn, xt, wst, acch, acct,
    qdl, dsend, drecv, qdb, accd, acdt, yz, prev, older, lz, nloc, etas, facs,
    mxs, mxa, mxb, mxc,
    s_pay, r_pay, s_d, r_d, s_a, r_a, s_b, r_b, s_c, r_c,
):
    ix, iy = lax.axis_index("gx"), lax.axis_index("gy")
    xx, xy = ix // 8, ix % 8

    def near(p, q):
        return ((ix + 32 + p) % 32, (iy + 16 + q) % 16)

    def dev_a(k):
        return (ix, (iy + k) % 16)

    def dev_b(k):
        return (xx * 8 + (xy + k) % 8, iy)

    def dev_c(k):
        return (((xx + k) % 4) * 8 + xy, iy)

    barrier = pltpu.get_barrier_semaphore()

    def hello(dev, n):
        def body(k, c):
            pl.semaphore_signal(barrier, inc=1, device_id=dev(k), device_id_type=MESH)
            return c

        lax.fori_loop(1, n, body, 0)

    hello(dev_a, 16)
    hello(dev_b, 8)
    hello(dev_c, 4)
    for p, q in DIRECTIONS:
        if p:
            pl.semaphore_signal(barrier, inc=1, device_id=near(p, q), device_id_type=MESH)

    for j in range(BLOCKS):
        for n, ref in enumerate((pos, mom_r, bfl_r)):
            pk[pl.ds(48 * n + j, 3, stride=16), :] = ref[:, TILE * j : TILE * (j + 1)]

    def packed(n):
        return pk[16 * n : 16 * (n + 1), :]

    ixf = ix.astype(F32)
    iyf = iy.astype(F32)
    rho = rho_r[...]
    x = [packed(0), packed(1), packed(2)]
    mom = [packed(3), packed(4), packed(5)]
    bfl = [packed(6), packed(7), packed(8)]
    psi = psi_r[...]
    speed = jnp.sqrt(1.0 + (bfl[0] * bfl[0] + bfl[1] * bfl[1] + bfl[2] * bfl[2]) / rho)
    facs[...] = amb_r[...] / (rho * jnp.sqrt(rho))
    mxs[0] = jnp.max(speed, axis=0, keepdims=True)
    live = jnp.ones_like(rho)
    zero = jnp.zeros_like(rho)
    for r, v in enumerate([*x, live, rho, *mom, *bfl, psi, speed, zero, zero, zero]):
        pay[pl.ds(r, 16, stride=16), :] = v

    pl.semaphore_wait(barrier, 15 + 7 + 3 + 6)

    def ring(dev, n, src, dst, ss, rs):
        def one(k):
            return pltpu.make_async_remote_copy(
                src_ref=mxs.at[src], dst_ref=dst.at[k], send_sem=ss.at[k], recv_sem=rs.at[k],
                device_id=dev(k), device_id_type=MESH,
            )

        def send():
            lax.fori_loop(1, n, lambda k, c: (one(k).start(), c)[1], 0)

        def wait():
            def body(k, c):
                one(k).wait_send()
                one(k).wait_recv()
                return c

            lax.fori_loop(1, n, body, 0)
            return lax.fori_loop(1, n, lambda k, c: jnp.maximum(c, dst[k]), mxs[src])

        return send, wait

    send_a, wait_a = ring(dev_a, 16, 0, mxa, s_a, r_a)
    send_b, wait_b = ring(dev_b, 8, 1, mxb, s_b, r_b)
    send_c, wait_c = ring(dev_c, 4, 2, mxc, s_c, r_c)
    send_a()

    gi = gi_r[...]
    for o in range(GBLOCKS):
        row = jnp.broadcast_to(gi[o : o + 1, :], (8, TILE))
        lane_b[o] = row & 127
        blk_b[o] = row >> 7

    lanes = lax.broadcasted_iota(jnp.int32, (8, TILE), 1)

    def gathered(load):
        def body(s, got):
            src = load(s)
            new = []
            for o in range(GBLOCKS):
                val = jnp.take_along_axis(src, lane_b[o], axis=1, mode="promise_in_bounds")
                new.append(jnp.where(blk_b[o] == s, val, got[o]))
            return tuple(new)

        return lax.fori_loop(0, BLOCKS, body, tuple(jnp.zeros((8, TILE), F32) for _ in range(GBLOCKS)))

    def shifted(got):
        out = []
        for d, k, lo, hi in PIECES:
            shift = STARTS[d] - STARTS[7 - d]
            a, s = shift // TILE, shift % TILE
            if lo >= s:
                out.append(pltpu.roll(got[k - a], s, 1) if s else got[k - a])
            elif hi <= s:
                out.append(pltpu.roll(got[k - a - 1], s, 1))
            else:
                out.append(
                    jnp.where(lanes >= s, pltpu.roll(got[k - a], s, 1), pltpu.roll(got[k - a - 1], s, 1))
                )
        return out

    exists = []
    for p, q in DIRECTIONS:
        e = (ix + p >= 0) & (ix + p < 32) & (iy + q >= 0) & (iy + q < 16)
        exists.append(e)

    def combined(load):
        out = []
        for k in range(GBLOCKS):
            tile = jnp.zeros((8, TILE), F32)
            for n, (d, kk, lo, hi) in enumerate(PIECES):
                if kk == k:
                    mask = (lanes >= lo) & (lanes < hi) & exists[d]
                    tile = jnp.where(mask, load(n), tile)
            out.append(tile)
        return out

    def copies(src, dst, ss, rs):
        out = []
        for d, (p, q) in enumerate(DIRECTIONS):
            part = pl.ds(OFFSET[d], COUNT[d])
            out.append(
                pltpu.make_async_remote_copy(
                    src_ref=src.at[part], dst_ref=dst.at[part], send_sem=ss.at[d], recv_sem=rs.at[d],
                    device_id=near(-p, -q), device_id_type=MESH,
                )
            )
        return out

    for g in range(2):
        got = gathered(lambda s, g=g: pay[pl.ds(pl.multiple_of(16 * s + 8 * g, 8), 8), :])
        for n, v in enumerate(shifted(got)):
            paysend[n, 8 * g : 8 * (g + 1), :] = v
    pay_copies = copies(paysend, payrecv, s_pay, r_pay)
    for c in pay_copies:
        c.start()

    def put_q(rows, base):
        for r, v in enumerate(rows):
            qt[pl.ds(base * QROWS + r, 16, stride=QROWS), :] = v

    qloc = q_rows([x[0] - ixf, x[1] - iyf, x[2]], live, rho, mom, bfl, psi, speed)
    for r, v in enumerate(qloc):
        qp[r] = v
    put_q([*qloc, zero, zero], 0)

    mxs[1] = wait_a()
    send_b()

    def put_x(j):
        tile = qt[pl.ds(pl.multiple_of(j * QROWS, 8), 8), :]
        xn[j] = tile
        xt[j] = jnp.transpose(tile)

    def split(j):
        v = qt[pl.ds(pl.multiple_of(j * QROWS, 8), QROWS), :]
        hi = v.astype(BF16).astype(F32)
        qb[j] = jnp.concatenate([hi, v - hi], axis=0).astype(BF16)

    def prep(j, c):
        put_x(j)
        split(j)
        return c

    lax.fori_loop(0, BLOCKS, prep, 0)
    mxs[2] = wait_b()
    send_c()

    for c in pay_copies:
        c.wait_recv()
    for g in range(2):
        tiles = combined(lambda n, g=g: payrecv[n, 8 * g : 8 * (g + 1), :])
        for k, v in enumerate(tiles):
            ghp[16 * k + 8 * g : 16 * k + 8 * g + 8, :] = v
    gh = [ghp[pl.ds(r, 16, stride=16), :] for r in range(13)]
    glive = gh[3]
    grho = jnp.where(glive > 0.0, gh[4], 1.0)
    gq = q_rows(
        [glive * (gh[0] - ixf), glive * (gh[1] - iyf), gh[2]], glive, grho, gh[5:8], gh[8:11], gh[11], gh[12]
    )
    gq = [jnp.where(glive > 0.0, v, 0.0) for v in gq]
    put_q([*gq, zero, zero], BLOCKS)
    lax.fori_loop(BLOCKS, BLOCKS + GBLOCKS, prep, 0)

    def fold(run, part, same):
        return part + jnp.where(same == 1, run, 0.0)

    def hydro_tile(t, run):
        i, j = tab[t], tab[64 + t]
        a, b = xn[i], xt[j]
        d0 = a[1:2, :] - b[:, 1:2]
        d1 = a[2:3, :] - b[:, 2:3]
        d2 = a[3:4, :] - b[:, 3:4]
        base = jnp.maximum(1.0 - 4.0 * (d0 * d0 + d1 * d1 + d2 * d2), 0.0)
        w = base * base
        hi = w.astype(BF16)
        lo = (w - hi.astype(F32)).astype(BF16)
        w2 = jnp.concatenate([hi, lo], axis=0)
        wst[t] = w2
        q = qb[j]
        part = jnp.dot(jnp.concatenate([q, q], axis=1), w2, preferred_element_type=F32)
        run = fold(run, part[:QROWS] + part[QROWS:], tab[128 + t])
        acch[t] = run
        return run

    def unrolled(body, n, start, by):
        def step(s, c):
            for u in range(by):
                c = body(s * by + u, c)
            return c

        return lax.fori_loop(0, n // by, step, start)

    acch[TILES] = jnp.zeros((QROWS, TILE), F32)
    accd[TILES] = jnp.zeros((8, TILE), F32)
    unrolled(hydro_tile, TILES, jnp.zeros((QROWS, TILE), F32), 4)
    for i in range(BLOCKS):
        acct[QROWS * i : QROWS * (i + 1), :] = acch[tab[192 + i]]

    chm = jnp.max(wait_c(), axis=1, keepdims=True)
    ch = jnp.broadcast_to(chm, (BLOCKS, TILE))
    dt = COURANT / ch

    acc = [acct[pl.ds(r, 16, stride=QROWS), :] for r in range(38)]
    qloc = [qp[r] for r in range(38)]
    fl, af = flux_of(qloc), flux_of(acc)
    n = acc[0]
    s_d_rows = [acc[1 + d] - qloc[1 + d] * n for d in range(3)]
    inv = 0.5 / (1.0 + n)
    rates = []
    for r in range(8):
        central = acc[30 + r]
        for d in range(3):
            central = central + fl[d][r] * s_d_rows[d] - qloc[1 + d] * af[d][r]
        if r == 7:
            central = ch * ch * central
        dissip = qloc[20] * (acc[4 + r] - qloc[4 + r] * n) + acc[12 + r] - qloc[4 + r] * acc[20]
        rates.append((dissip - central) * inv)
    nloc[0] = n
    nloc[1] = inv
    nloc[2] = dt
    rho_o[...] = qloc[4] + dt * rates[0]
    psi_o[...] = (qloc[11] + dt * rates[7]) * jnp.exp(-DAMPING * dt * ch)
    for d in range(3):
        pk[16 * d : 16 * (d + 1), :] = qloc[5 + d] + dt * rates[1 + d]
        y = qloc[8 + d] + dt * rates[4 + d]
        yz[d] = y
        prev[d] = y
        older[d] = y
        lz[d] = zero
    for j in range(BLOCKS):
        mom_o[:, TILE * j : TILE * (j + 1)] = pk[pl.ds(j, 3, stride=16), :]
    qdl[pl.ds(7, 16, stride=8), :] = zero

    table = rkl_table(SECTIONS)

    def dsplit(v):
        hi = v.astype(BF16).astype(F32)
        return jnp.concatenate([hi, v - hi], axis=0).astype(BF16)

    def section(k, c):
        def coef(m):
            val = jnp.asarray(table[0][m], F32)
            for j in range(1, SECTIONS):
                val = jnp.where(k == j, jnp.asarray(table[j][m], F32), val)
            return val

        mu, nu, c0, mut, gam = (coef(m) for m in range(5))
        y = [prev[d] for d in range(3)]
        eta = ohm_r[...] + facs[...] * (y[0] * y[0] + y[1] * y[1] + y[2] * y[2])
        for r, v in enumerate([*y, *[eta * u for u in y], eta]):
            qdl[pl.ds(r, 16, stride=8), :] = v
        got = gathered(lambda s: qdl[pl.ds(pl.multiple_of(8 * s, 8), 8), :])
        for m, v in enumerate(shifted(got)):
            dsend[k, m] = v
        cps = copies(dsend.at[k], drecv.at[k], s_d.at[k], r_d.at[k])
        for cp in cps:
            cp.start()
        for j in range(BLOCKS):
            qdb[j] = dsplit(qdl[8 * j : 8 * j + 8, :])
        for cp in cps:
            cp.wait_recv()
        for m, v in enumerate(combined(lambda m: drecv[k, m])):
            qdb[BLOCKS + m] = dsplit(v)

        def tile(t, run):
            q = qdb[tab[64 + t]]
            part = jnp.dot(jnp.concatenate([q, q], axis=1), wst[t], preferred_element_type=F32)
            run = fold(run, part[:8] + part[8:], tab[128 + t])
            accd[t] = run
            return run

        unrolled(tile, TILES, jnp.zeros((8, TILE), F32), 8)
        for i in range(BLOCKS):
            acdt[8 * i : 8 * (i + 1), :] = accd[tab[192 + i]]
        acc = [acdt[pl.ds(r, 16, stride=8), :] for r in range(7)]
        n, inv, dt = nloc[0], nloc[1], nloc[2]
        for d in range(3):
            rate = (eta * (acc[d] - y[d] * n) + acc[3 + d] - y[d] * acc[6]) * inv
            lzero = jnp.where(k == 0, rate, lz[d])
            lz[d] = lzero
            nxt = mu * y[d] + nu * older[d] + c0 * yz[d] + dt * (mut * rate + gam * lzero)
            older[d] = y[d]
            prev[d] = nxt
        for cp in cps:
            cp.wait_send()
        return c

    lax.fori_loop(0, SECTIONS, section, 0)
    for d in range(3):
        pk[16 * d : 16 * (d + 1), :] = prev[d]
    for j in range(BLOCKS):
        bfl_o[:, TILE * j : TILE * (j + 1)] = pk[pl.ds(j, 3, stride=16), :]
    for c in pay_copies:
        c.wait_send()


def tile_table(tile_i, tile_j, tile_count):
    order = jnp.arange(TILES, dtype=jnp.int32)
    used = order < tile_count[0]
    key = jnp.where(used, tile_i * 32 + tile_j, 1024 + order)
    rank = jnp.sum((key[None, :] < key[:, None]).astype(jnp.int32), axis=1)
    put = rank[:, None] == order[None, :]
    skey = jnp.sum(jnp.where(put, key[:, None], 0), axis=0)
    before = jnp.sum(jnp.where(put, 0, 0), axis=0)
    valid = skey < 1024
    si = jnp.where(valid, skey >> 5, 0)
    sj = jnp.where(valid, skey & 31, 0)
    prior = jnp.concatenate([jnp.full((1,), -1, jnp.int32), si[:-1]])
    same = (si == prior).astype(jnp.int32) + before
    blocks = jnp.arange(BLOCKS, dtype=jnp.int32)
    mine = used[None, :] & (tile_i[None, :] == blocks[:, None])
    upto = used[None, :] & (tile_i[None, :] <= blocks[:, None])
    total = jnp.sum(mine.astype(jnp.int32), axis=1)
    last = jnp.where(total > 0, jnp.sum(upto.astype(jnp.int32), axis=1) - 1, TILES)
    return jnp.concatenate([si, sj, same, last, jnp.zeros((48,), jnp.int32)])


def shards(
    positions, density, momentum, field, psi, ohmic, ambipolar, ghost_index, tile_i, tile_j, tile_count
):
    table = tile_table(tile_i, tile_j, tile_count)
    gi = jnp.concatenate([ghost_index, jnp.zeros((2048 - 1088,), jnp.int32)]).reshape(16, TILE)

    def two(v):
        return v.reshape(BLOCKS, TILE)

    vmem = pl.BlockSpec(memory_space=pltpu.VMEM)
    V = pltpu.VMEM
    D = pltpu.SemaphoreType.DMA
    out = pl.pallas_call(
        kernel,
        out_shape=(
            jax.ShapeDtypeStruct((BLOCKS, TILE), F32),
            jax.ShapeDtypeStruct((3, 2048), F32),
            jax.ShapeDtypeStruct((3, 2048), F32),
            jax.ShapeDtypeStruct((BLOCKS, TILE), F32),
        ),
        in_specs=[pl.BlockSpec(memory_space=pltpu.SMEM)] + [vmem] * 8,
        out_specs=(vmem,) * 4,
        scratch_shapes=[
            V((144, TILE), F32),
            V((GBLOCKS, 8, TILE), jnp.int32),
            V((GBLOCKS, 8, TILE), jnp.int32),
            V((256, TILE), F32),
            V((NPIECE, 16, TILE), F32),
            V((NPIECE, 16, TILE), F32),
            V((256, TILE), F32),
            V((QROWS, BLOCKS, TILE), F32),
            V((32 * QROWS, TILE), F32),
            V((25, 2 * QROWS, TILE), BF16),
            V((25, 8, TILE), F32),
            V((25, TILE, 8), F32),
            V((TILES, 2 * TILE, TILE), BF16),
            V((TILES + 1, QROWS, TILE), F32),
            V((BLOCKS * QROWS, TILE), F32),
            V((BLOCKS * 8, TILE), F32),
            V((SECTIONS, NPIECE, 8, TILE), F32),
            V((SECTIONS, NPIECE, 8, TILE), F32),
            V((25, 16, TILE), BF16),
            V((TILES + 1, 8, TILE), F32),
            V((BLOCKS * 8, TILE), F32),
            V((3, BLOCKS, TILE), F32),
            V((3, BLOCKS, TILE), F32),
            V((3, BLOCKS, TILE), F32),
            V((3, BLOCKS, TILE), F32),
            V((3, BLOCKS, TILE), F32),
            V((BLOCKS, TILE), F32),
            V((BLOCKS, TILE), F32),
            V((3, 1, TILE), F32),
            V((16, 1, TILE), F32),
            V((8, 1, TILE), F32),
            V((4, 1, TILE), F32),
            D((8,)), D((8,)), D((SECTIONS, 8)), D((SECTIONS, 8)),
            D((16,)), D((16,)), D((8,)), D((8,)), D((4,)), D((4,)),
        ],
        compiler_params=pltpu.CompilerParams(
            collective_id=0, has_side_effects=True, vmem_limit_bytes=40 * 1024 * 1024
        ),
    )(table, positions, two(density), momentum, field, two(psi), two(ohmic), two(ambipolar), gi)
    return out[0].reshape(-1), out[1], out[2], out[3].reshape(-1)


def solution(mesh):
    one, three = P(("gx", "gy")), P(None, ("gx", "gy"))
    return jax.shard_map(
        shards,
        mesh=mesh,
        in_specs=(three, one, three, three, one, one, one, one, one, one, one),
        out_specs=(one, three, three, one),
        check_vma=False,
    )
```

```python
import jax
import jax.numpy as jnp
from jax import lax
from jax.experimental import pallas as pl
from jax.experimental.pallas import tpu as pltpu
from jax.sharding import PartitionSpec as P

TILE = 128
SECTIONS = 4
SIZES = [32, 320, 32, 160, 160, 32, 320, 32]
DIRECTIONS = [(-1, -1), (-1, 0), (-1, 1), (0, -1), (0, 1), (1, -1), (1, 0), (1, 1)]
STARTS = [sum(SIZES[:d]) for d in range(8)]
BLOCKS = 16
GBLOCKS = 9
TILES = 64
COURANT = 0.3
DAMPING = 0.5
MESH = pl.DeviceIdType.MESH
F32 = jnp.float32
BF16 = jnp.bfloat16

PIECES = []
OFFSET = []
for d in range(8):
    OFFSET.append(len(PIECES))
    for k in range(STARTS[d] // TILE, (STARTS[d] + SIZES[d] - 1) // TILE + 1):
        lo = max(STARTS[d] - k * TILE, 0)
        hi = min(STARTS[d] + SIZES[d] - k * TILE, TILE)
        PIECES.append((d, k, lo, hi))
COUNT = [sum(1 for p in PIECES if p[0] == d) for d in range(8)]
NPIECE = len(PIECES)

QROWS = 40


def rkl_table(sections):
    wfirst = 4.0 / (sections * sections + sections - 2)
    bvals = [1.0 / 3.0] * 3 + [(j * j + j - 2) / (2.0 * j * (j + 1)) for j in range(3, sections + 1)]
    rows = [(1.0, 0.0, 0.0, bvals[1] * wfirst, 0.0)]
    for j in range(2, sections + 1):
        mu = (2.0 * j - 1.0) / j * bvals[j] / bvals[j - 1]
        nu = -(j - 1.0) / j * bvals[j] / bvals[j - 2]
        mut = mu * wfirst
        rows.append((mu, nu, 1.0 - mu - nu, mut, -(1.0 - bvals[j - 1]) * mut))
    return rows


def q_rows(x, live, rho, mom, bfl, psi, speed):
    inv = 1.0 / rho
    vel = [m * inv for m in mom]
    ptot = rho + 0.5 * (bfl[0] * bfl[0] + bfl[1] * bfl[1] + bfl[2] * bfl[2])
    state = [rho, *mom, *bfl, psi]
    t = {}
    for a in range(3):
        for b in range(a, 3):
            v = mom[b] * vel[a] - bfl[b] * bfl[a]
            t[a, b] = t[b, a] = v + ptot if a == b else v
    ind = {}
    for a in range(3):
        for b in range(a + 1, 3):
            ind[a, b] = vel[a] * bfl[b] - bfl[a] * vel[b]
    gsum = [x[0] * mom[0] + x[1] * mom[1] + x[2] * mom[2]]
    for k in range(3):
        gsum.append(x[0] * t[0, k] + x[1] * t[1, k] + x[2] * t[2, k])
    gsum.append(x[0] * psi - x[1] * ind[0, 1] - x[2] * ind[0, 2])
    gsum.append(x[0] * ind[0, 1] + x[1] * psi - x[2] * ind[1, 2])
    gsum.append(x[0] * ind[0, 2] + x[1] * ind[1, 2] + x[2] * psi)
    gsum.append(x[0] * bfl[0] + x[1] * bfl[1] + x[2] * bfl[2])
    return [
        live, *x, *state, *[speed * u for u in state], speed,
        t[0, 0], t[0, 1], t[0, 2], t[1, 1], t[1, 2], t[2, 2],
        ind[0, 1], ind[0, 2], ind[1, 2], *gsum,
    ]


def flux_of(q):
    m, b, psi = q[5:8], q[8:11], q[11]
    t = {(0, 0): q[21], (0, 1): q[22], (0, 2): q[23], (1, 1): q[24], (1, 2): q[25], (2, 2): q[26]}
    i01, i02, i12 = q[27:30]
    ind = [[psi, i01, i02], [-i01, psi, i12], [-i02, -i12, psi]]
    return [[m[d], *[t[min(d, k), max(d, k)] for k in range(3)], *ind[d], b[d]] for d in range(3)]


def kernel(
    pos_h, rho_h, mom_h, bfl_h, psi_h, ohm_h, amb_h, gi_h, ti_h, tj_h, cnt_h,
    rho_o, mom_o, bfl_o, psi_o,
    pos_r, rho_r, mom_r, bfl_r, psi_r, ohm_r, amb_r, gi_r, gis_r, ti_r, tj_r, cnt_r, tabv, tab,
    pk, lane_b, blk_b, pay, paysend, payrecv, ghp, qp, qt, qb, xn, xb, wst, acch, acct,
    gsrc, qdl, dsend, drecv, qdb, accd, acdt, yz, older, lz, nloc, facs,
    mxs, mxa, mxb, mxc,
    s_in, s_tab, s_pay, r_pay, s_d, r_d, s_a, r_a, s_b, r_b, s_c, r_c,
):
    ix, iy = lax.axis_index("gx"), lax.axis_index("gy")
    xx, xy = ix // 8, ix % 8

    def near(p, q):
        return ((ix + 32 + p) % 32, (iy + 16 + q) % 16)

    def dev_a(k):
        return (ix, (iy + k) % 16)

    def dev_b(k):
        return (xx * 8 + (xy + k) % 8, iy)

    def dev_c(k):
        return (((xx + k) % 4) * 8 + xy, iy)

    loads = {}
    for n, (name, src, dst) in enumerate([
        ("bfl", bfl_h, bfl_r), ("rho", rho_h, rho_r), ("pos", pos_h, pos_r), ("mom", mom_h, mom_r),
        ("psi", psi_h, psi_r), ("ohm", ohm_h, ohm_r), ("amb", amb_h, amb_r),
        ("gi", gi_h.at[pl.ds(0, 1024)], gi_r), ("gis", gi_h.at[pl.ds(1024, 64)], gis_r),
        ("ti", ti_h, ti_r), ("tj", tj_h, tj_r), ("cnt", cnt_h, cnt_r),
    ]):
        loads[name] = pltpu.make_async_copy(src, dst, s_in.at[n])
        loads[name].start()

    barrier = pltpu.get_barrier_semaphore()

    def hello(dev, n):
        def body(k, c):
            pl.semaphore_signal(barrier, inc=1, device_id=dev(k), device_id_type=MESH)
            return c

        lax.fori_loop(1, n, body, 0)

    hello(dev_a, 16)
    hello(dev_b, 8)
    hello(dev_c, 4)
    for p, q in DIRECTIONS:
        if p:
            pl.semaphore_signal(barrier, inc=1, device_id=near(p, q), device_id_type=MESH)

    def pack(n, ref):
        for j in range(BLOCKS):
            pk[pl.ds(48 * n + j, 3, stride=16), :] = ref[:, TILE * j : TILE * (j + 1)]
        return [pk[48 * n + 16 * d : 48 * n + 16 * (d + 1), :] for d in range(3)]

    def unpack(n, ref):
        for j in range(BLOCKS):
            ref[:, TILE * j : TILE * (j + 1)] = pk[pl.ds(48 * n + j, 3, stride=16), :]

    ixf = ix.astype(F32)
    iyf = iy.astype(F32)
    loads["bfl"].wait()
    loads["rho"].wait()
    rho = rho_r[...]
    bfl = pack(2, bfl_r)
    speed = jnp.sqrt(1.0 + (bfl[0] * bfl[0] + bfl[1] * bfl[1] + bfl[2] * bfl[2]) / rho)
    mxs[0] = jnp.max(speed, axis=0, keepdims=True)

    pl.semaphore_wait(barrier, 15 + 7 + 3 + 6)

    def ring(dev, n, src, dst, ss, rs):
        def one(k):
            return pltpu.make_async_remote_copy(
                src_ref=mxs.at[src], dst_ref=dst.at[k], send_sem=ss.at[k], recv_sem=rs.at[k],
                device_id=dev(k), device_id_type=MESH,
            )

        def send():
            lax.fori_loop(1, n, lambda k, c: (one(k).start(), c)[1], 0)

        def wait():
            def body(k, c):
                one(k).wait_send()
                one(k).wait_recv()
                return c

            lax.fori_loop(1, n, body, 0)
            return lax.fori_loop(1, n, lambda k, c: jnp.maximum(c, dst[k]), mxs[src])

        return send, wait

    send_a, wait_a = ring(dev_a, 16, 0, mxa, s_a, r_a)
    send_b, wait_b = ring(dev_b, 8, 1, mxb, s_b, r_b)
    send_c, wait_c = ring(dev_c, 4, 2, mxc, s_c, r_c)
    send_a()

    for name in ("pos", "mom", "psi", "ohm", "amb", "gi", "gis", "ti", "tj", "cnt"):
        loads[name].wait()
    x = pack(0, pos_r)
    mom = pack(1, mom_r)
    psi = psi_r[...]
    fac = amb_r[...] / (rho * jnp.sqrt(rho))
    facs[...] = fac
    live = jnp.ones_like(rho)
    zero = jnp.zeros_like(rho)
    for r, v in enumerate([*bfl, live, *mom, rho, *x, psi, speed, ohm_r[...], fac, zero]):
        pay[pl.ds(r, 16, stride=16), :] = v

    lanes = lax.broadcasted_iota(jnp.int32, (8, TILE), 1)

    def vector_of(scalar, n):
        v = jnp.zeros((8, TILE), jnp.int32)
        for m in range(n):
            v = jnp.where(lanes == m, scalar(m), v)
        return v

    for o in range(GBLOCKS):
        if o < 8:
            row = jnp.broadcast_to(gi_r[TILE * o : TILE * (o + 1)].reshape(1, TILE), (8, TILE))
        else:
            row = vector_of(lambda m: gis_r[m], 64)
        lane_b[o] = row & 127
        blk_b[o] = row >> 7

    def gathered(load):
        got = [jnp.zeros((8, TILE), F32) for _ in range(GBLOCKS)]
        for s in range(BLOCKS):
            src = load(s)
            for o in range(GBLOCKS):
                val = jnp.take_along_axis(src, lane_b[o], axis=1, mode="promise_in_bounds")
                got[o] = jnp.where(blk_b[o] == s, val, got[o])
        return got

    upper = lax.broadcasted_iota(jnp.int32, (8, TILE), 0) < 4

    def gathered4(rows):
        for r, v in enumerate(rows):
            gsrc[pl.ds(r, 8, stride=8), :] = v[:8]
            gsrc[pl.ds(4 + r, 8, stride=8), :] = v[8:]
        half = jnp.where(upper, 0, 8)
        got = [jnp.zeros((8, TILE), F32) for _ in range(GBLOCKS)]
        for o in range(GBLOCKS):
            lane, blk = lane_b[o], blk_b[o] - half
            for s in range(8):
                val = jnp.take_along_axis(gsrc[8 * s : 8 * s + 8, :], lane, axis=1, mode="promise_in_bounds")
                got[o] = jnp.where(blk == s, val, got[o])
        return [v + pltpu.roll(v, 4, 0) for v in got]

    def shifted(got):
        out = []
        for d, k, lo, hi in PIECES:
            shift = STARTS[d] - STARTS[7 - d]
            a, s = shift // TILE, shift % TILE
            if lo >= s:
                out.append(pltpu.roll(got[k - a], s, 1) if s else got[k - a])
            elif hi <= s:
                out.append(pltpu.roll(got[k - a - 1], s, 1))
            else:
                out.append(
                    jnp.where(lanes >= s, pltpu.roll(got[k - a], s, 1), pltpu.roll(got[k - a - 1], s, 1))
                )
        return out

    exists = []
    for p, q in DIRECTIONS:
        e = (ix + p >= 0) & (ix + p < 32) & (iy + q >= 0) & (iy + q < 16)
        exists.append(e)

    def combined(load):
        out = []
        for k in range(GBLOCKS):
            tile = jnp.zeros((8, TILE), F32)
            for n, (d, kk, lo, hi) in enumerate(PIECES):
                if kk == k:
                    mask = (lanes >= lo) & (lanes < hi) & exists[d]
                    tile = jnp.where(mask, load(n), tile)
            out.append(tile)
        return out

    def copies(src, dst, ss, rs):
        out = []
        for d, (p, q) in enumerate(DIRECTIONS):
            part = pl.ds(OFFSET[d], COUNT[d])
            out.append(
                pltpu.make_async_remote_copy(
                    src_ref=src.at[part], dst_ref=dst.at[part], send_sem=ss.at[d], recv_sem=rs.at[d],
                    device_id=near(-p, -q), device_id_type=MESH,
                )
            )
        return out

    for g in range(2):
        got = gathered(lambda s, g=g: pay[16 * s + 8 * g : 16 * s + 8 * g + 8, :])
        for n, v in enumerate(shifted(got)):
            paysend[n, 8 * g : 8 * (g + 1), :] = v
    pay_copies = copies(paysend, payrecv, s_pay, r_pay)
    for c in pay_copies:
        c.start()

    mxs[1] = wait_a()
    send_b()

    def put_q(rows, base):
        for r, v in enumerate(rows):
            qt[pl.ds(base * QROWS + r, 16, stride=QROWS), :] = v

    qloc = q_rows([x[0] - ixf, x[1] - iyf, x[2]], live, rho, mom, bfl, psi, speed)
    for r, v in enumerate(qloc):
        qp[r] = v
    put_q([*qloc, zero, zero], 0)

    def put_x(j):
        tile = qt[pl.ds(pl.multiple_of(j * QROWS, 8), 8), :]
        xn[j] = tile
        col = jnp.transpose(tile)
        for d in range(3):
            xb[j, d] = jnp.broadcast_to(col[:, 1 + d : 2 + d], (TILE, TILE))

    def split(j):
        v = qt[pl.ds(pl.multiple_of(j * QROWS, 8), QROWS), :]
        hi = v.astype(BF16).astype(F32)
        qb[j] = jnp.concatenate([hi, v - hi], axis=0).astype(BF16)

    def prep(j, c):
        put_x(j)
        split(j)
        return c

    lax.fori_loop(0, BLOCKS, prep, 0)

    row8 = (8, TILE)
    lane = lax.broadcasted_iota(jnp.int32, row8, 1)
    used = lane < jnp.minimum(cnt_r[0], TILES)
    pair = vector_of(lambda m: ti_r[m] * 32 + tj_r[m], TILES)
    key = jnp.where(used, pair, 1024 + lane)
    keycol = jnp.broadcast_to(jnp.transpose(key)[:, 0:1], (TILE, TILE))
    keyrow = jnp.broadcast_to(key[0:1, :], (TILE, TILE))
    rank = jnp.sum(jnp.where(keycol < keyrow, 1, 0), axis=0, keepdims=True)
    rank = jnp.broadcast_to(jnp.transpose(jnp.broadcast_to(rank, row8))[:, 0:1], (TILE, TILE))
    lanes2 = lax.broadcasted_iota(jnp.int32, (TILE, TILE), 1)
    skey = jnp.sum(jnp.where(rank == lanes2, keycol, 0), axis=0, keepdims=True)
    total = jnp.sum(jnp.where(keycol < (lanes2 + 1) * 32, 1, 0), axis=0, keepdims=True)
    below = jnp.sum(jnp.where(keycol < lanes2 * 32, 1, 0), axis=0, keepdims=True)
    last = jnp.where(total > below, total - 1, TILES)
    skey = jnp.broadcast_to(skey, row8)
    valid = skey < 1024
    si = jnp.where(valid, skey >> 5, 0)
    sj = jnp.where(valid, skey & 31, 0)
    same = jnp.where((lane > 0) & (si == pltpu.roll(si, 1, 1)), 1, 0)
    sub = lax.broadcasted_iota(jnp.int32, row8, 0)
    tabv[...] = jnp.where(sub == 0, si, jnp.where(sub == 1, sj, jnp.where(sub == 2, same, last)))
    to_smem = pltpu.make_async_copy(tabv, tab, s_tab)
    to_smem.start()

    mxs[2] = wait_b()
    send_c()

    for c in pay_copies:
        c.wait_recv()
    for g in range(2):
        tiles = combined(lambda n, g=g: payrecv[n, 8 * g : 8 * (g + 1), :])
        for k, v in enumerate(tiles):
            ghp[16 * k + 8 * g : 16 * k + 8 * g + 8, :] = v
    gh = [ghp[pl.ds(r, 16, stride=16), :] for r in range(13)]
    glive = gh[3]
    grho = jnp.where(glive > 0.0, gh[7], 1.0)
    gq = q_rows(
        [glive * (gh[8] - ixf), glive * (gh[9] - iyf), gh[10]], glive, grho, gh[4:7], gh[0:3], gh[11], gh[12]
    )
    gq = [jnp.where(glive > 0.0, v, 0.0) for v in gq]
    put_q([*gq, zero, zero], BLOCKS)
    lax.fori_loop(BLOCKS, BLOCKS + GBLOCKS, prep, 0)

    def inside(index, n):
        return jnp.minimum(jnp.maximum(index, 0), n - 1)

    def fold(run, part, same):
        return part + jnp.where(same == 1, run, 0.0)

    def hydro_tile(t, run):
        i, j = inside(tab[0, t], BLOCKS), inside(tab[1, t], BLOCKS + GBLOCKS)
        a = xn[i]
        d0 = a[1:2, :] - xb[j, 0]
        d1 = a[2:3, :] - xb[j, 1]
        d2 = a[3:4, :] - xb[j, 2]
        base = jnp.maximum(1.0 - 4.0 * (d0 * d0 + d1 * d1 + d2 * d2), 0.0)
        w = base * base
        hi = w.astype(BF16)
        lo = (w - hi.astype(F32)).astype(BF16)
        w2 = jnp.concatenate([hi, lo], axis=0)
        wst[t] = w2
        q = qb[j]
        part = jnp.dot(jnp.concatenate([q, q], axis=1), w2, preferred_element_type=F32)
        run = fold(run, part[:QROWS] + part[QROWS:], tab[2, t])
        acch[t] = run
        return run

    def unrolled(body, n, start, by):
        def step(s, c):
            for u in range(by):
                c = body(s * by + u, c)
            return c

        return lax.fori_loop(0, n // by, step, start)

    to_smem.wait()
    acch[TILES] = jnp.zeros((QROWS, TILE), F32)
    accd[TILES] = jnp.zeros((8, TILE), F32)
    unrolled(hydro_tile, TILES, jnp.zeros((QROWS, TILE), F32), 4)
    for i in range(BLOCKS):
        acct[QROWS * i : QROWS * (i + 1), :] = acch[inside(tab[3, i], TILES + 1)]

    acc = [acct[pl.ds(r, 16, stride=QROWS), :] for r in range(38)]
    qloc = [qp[r] for r in range(38)]
    fl, af = flux_of(qloc), flux_of(acc)
    n = acc[0]
    s_d_rows = [acc[1 + d] - qloc[1 + d] * n for d in range(3)]
    inv = 0.5 / (1.0 + n)
    rates = []
    for r in range(8):
        central = acc[30 + r]
        for d in range(3):
            central = central + fl[d][r] * s_d_rows[d] - qloc[1 + d] * af[d][r]
        if r == 7:
            psi_central = central
            central = 0.0
        dissip = qloc[20] * (acc[4 + r] - qloc[4 + r] * n) + acc[12 + r] - qloc[4 + r] * acc[20]
        rates.append((dissip - central) * inv)

    sub = lax.broadcasted_iota(jnp.int32, (8, TILE), 0)

    def exchange(k, rows):
        for m, v in enumerate(shifted(gathered4(rows))):
            dsend[k, m] = v
        cps = copies(dsend.at[k], drecv.at[k], s_d.at[k], r_d.at[k])
        for cp in cps:
            cp.start()
        return cps

    def dsplit(v):
        hi = v.astype(BF16).astype(F32)
        return jnp.concatenate([hi, v - hi], axis=0).astype(BF16)

    def put_local(y, eta):
        for r, v in enumerate([*y, eta, *[eta * u for u in y], zero]):
            qdl[pl.ds(r, 16, stride=8), :] = v
        for j in range(BLOCKS):
            qdb[j] = dsplit(qdl[8 * j : 8 * j + 8, :])

    def put_ghost(m, v):
        eta = jnp.broadcast_to(v[3:4, :], (8, TILE))
        qdb[BLOCKS + m] = dsplit(v * jnp.where(upper, 1.0, jnp.where(sub < 7, eta, 0.0)))

    cps = exchange(0, [*rates[4:7], zero])

    chm = jnp.max(wait_c(), axis=1, keepdims=True)
    ch = jnp.broadcast_to(chm, (BLOCKS, TILE))
    dt = COURANT / ch
    dt8 = dt[:8]
    rho_o[...] = qloc[4] + dt * rates[0]
    psi_o[...] = (qloc[11] + dt * (rates[7] - ch * ch * psi_central * inv)) * jnp.exp(-DAMPING * dt * ch)
    for d in range(3):
        mom_o[16 * d : 16 * (d + 1), :] = qloc[5 + d] + dt * rates[1 + d]
        yz[d] = qloc[8 + d] + dt * rates[4 + d]
    nloc[0] = n
    nloc[1] = inv
    nloc[2] = dt
    table = rkl_table(SECTIONS)

    def eta_of(y):
        return ohm_r[...] + facs[...] * (y[0] * y[0] + y[1] * y[1] + y[2] * y[2])

    def fold_tiles():
        def tile(t, run):
            q = qdb[inside(tab[1, t], BLOCKS + GBLOCKS)]
            part = jnp.dot(jnp.concatenate([q, q], axis=1), wst[t], preferred_element_type=F32)
            run = fold(run, part[:8] + part[8:], tab[2, t])
            accd[t] = run
            return run

        unrolled(tile, TILES, jnp.zeros((8, TILE), F32), 16)
        for i in range(BLOCKS):
            acdt[8 * i : 8 * (i + 1), :] = accd[inside(tab[3, i], TILES + 1)]
        return [acdt[pl.ds(r, 16, stride=8), :] for r in range(7)]

    def rates_of(y, eta):
        acc = fold_tiles()
        n, inv = nloc[0], nloc[1]
        return [(eta * (acc[d] - y[d] * n) + acc[4 + d] - y[d] * acc[3]) * inv for d in range(3)]

    y = [yz[d] for d in range(3)]
    eta = eta_of(y)
    put_local(y, eta)
    for cp in cps:
        cp.wait_recv()
    for m, v in enumerate(combined(lambda m: drecv[0, m])):
        g0, g1 = ghp[16 * m : 16 * m + 8, :], ghp[16 * m + 8 : 16 * m + 16, :]
        y0 = jnp.where(sub < 3, g0 + dt8 * v, 0.0)
        sq = jnp.sum(y0 * y0, axis=0, keepdims=True)
        geta = g1[5:6, :] + g1[6:7, :] * sq
        w = jnp.where(sub == 3, jnp.broadcast_to(geta, (8, TILE)), y0)
        put_ghost(m, w + pltpu.roll(w, 4, 0))
    rate = rates_of(y, eta)
    mut = table[0][3]
    for d in range(3):
        lz[d] = rate[d]
        older[d] = y[d]
    y = [y[d] + mut * dt * rate[d] for d in range(3)]

    for k in range(1, SECTIONS):
        mu, nu, c0, mut, gam = table[k]
        eta = eta_of(y)
        cps += exchange(k, [*y, eta])
        put_local(y, eta)
        base = [mu * y[d] + nu * older[d] + c0 * yz[d] + gam * dt * lz[d] for d in range(3)]
        for d in range(3):
            older[d] = y[d]
        for cp in cps[8 * k :]:
            cp.wait_recv()
        for m, v in enumerate(combined(lambda m: drecv[k, m])):
            put_ghost(m, v)
        rate = rates_of(y, eta)
        y = [base[d] + mut * dt * rate[d] for d in range(3)]

    for d in range(3):
        bfl_o[16 * d : 16 * (d + 1), :] = y[d]
    for c in pay_copies + cps:
        c.wait_send()


def finish(rho_p, mom_p, bfl_p, psi_p, rho_h, mom_h, bfl_h, psi_h, mom_r, bfl_r, sems):
    first = [
        pltpu.make_async_copy(rho_p, rho_h, sems.at[0]),
        pltpu.make_async_copy(psi_p, psi_h, sems.at[1]),
    ]
    for c in first:
        c.start()
    for src, dst in ((mom_p, mom_r), (bfl_p, bfl_r)):
        for j in range(BLOCKS):
            dst[:, TILE * j : TILE * (j + 1)] = src[pl.ds(j, 3, stride=16), :]
    second = [
        pltpu.make_async_copy(mom_r, mom_h, sems.at[2]),
        pltpu.make_async_copy(bfl_r, bfl_h, sems.at[3]),
    ]
    for c in second:
        c.start()
    for c in first + second:
        c.wait()


def shards(
    positions, density, momentum, field, psi, ohmic, ambipolar, ghost_index, tile_i, tile_j, tile_count
):
    def pin(v):
        return pltpu.with_memory_space_constraint(v, pltpu.HBM) if v.shape[0] != 1 else v

    def two(v):
        return v.reshape(BLOCKS, TILE)

    vmem = pl.BlockSpec(memory_space=pltpu.VMEM)
    hbm = pl.BlockSpec(memory_space=pltpu.HBM)
    V = pltpu.VMEM
    I32 = jnp.int32
    D = pltpu.SemaphoreType.DMA
    out = pl.pallas_call(
        kernel,
        out_shape=(
            jax.ShapeDtypeStruct((BLOCKS, TILE), F32),
            jax.ShapeDtypeStruct((48, TILE), F32),
            jax.ShapeDtypeStruct((48, TILE), F32),
            jax.ShapeDtypeStruct((BLOCKS, TILE), F32),
        ),
        in_specs=[hbm] * 11,
        out_specs=(vmem,) * 4,
        scratch_shapes=[
            V((3, 2048), F32), V((16, TILE), F32), V((3, 2048), F32), V((3, 2048), F32),
            V((16, TILE), F32), V((16, TILE), F32), V((16, TILE), F32),
            V((1024,), I32), pltpu.SMEM((64,), I32), pltpu.SMEM((64,), I32), pltpu.SMEM((64,), I32), pltpu.SMEM((1,), I32),
            V((8, TILE), I32), pltpu.SMEM((8, TILE), I32),
            V((144, TILE), F32),
            V((GBLOCKS, 8, TILE), jnp.int32),
            V((GBLOCKS, 8, TILE), jnp.int32),
            V((256, TILE), F32),
            V((NPIECE, 16, TILE), F32),
            V((NPIECE, 16, TILE), F32),
            V((256, TILE), F32),
            V((QROWS, BLOCKS, TILE), F32),
            V((32 * QROWS, TILE), F32),
            V((25, 2 * QROWS, TILE), BF16),
            V((25, 8, TILE), F32),
            V((25, 3, TILE, TILE), F32),
            V((TILES, 2 * TILE, TILE), BF16),
            V((TILES + 1, QROWS, TILE), F32),
            V((BLOCKS * QROWS, TILE), F32),
            V((64, TILE), F32),
            V((BLOCKS * 8, TILE), F32),
            V((SECTIONS, NPIECE, 8, TILE), F32),
            V((SECTIONS, NPIECE, 8, TILE), F32),
            V((25, 16, TILE), BF16),
            V((TILES + 1, 8, TILE), F32),
            V((BLOCKS * 8, TILE), F32),
            V((3, BLOCKS, TILE), F32),
            V((3, BLOCKS, TILE), F32),
            V((3, BLOCKS, TILE), F32),
            V((3, BLOCKS, TILE), F32),
            V((BLOCKS, TILE), F32),
            V((3, 1, TILE), F32),
            V((16, 1, TILE), F32),
            V((8, 1, TILE), F32),
            V((4, 1, TILE), F32),
            D((12,)), D, D((8,)), D((8,)), D((SECTIONS, 8)), D((SECTIONS, 8)),
            D((16,)), D((16,)), D((8,)), D((8,)), D((4,)), D((4,)),
        ],
        compiler_params=pltpu.CompilerParams(
            collective_id=0, has_side_effects=True, vmem_limit_bytes=48 * 1024 * 1024
        ),
    )(*map(pin, [
        positions, two(density), momentum, field, two(psi), two(ohmic), two(ambipolar),
        ghost_index, tile_i, tile_j, tile_count,
    ]))
    out = pl.pallas_call(
        finish,
        out_shape=(
            jax.ShapeDtypeStruct((BLOCKS, TILE), F32),
            jax.ShapeDtypeStruct((3, 2048), F32),
            jax.ShapeDtypeStruct((3, 2048), F32),
            jax.ShapeDtypeStruct((BLOCKS, TILE), F32),
        ),
        in_specs=[vmem] * 4,
        out_specs=(hbm,) * 4,
        scratch_shapes=[V((3, 2048), F32), V((3, 2048), F32), D((4,))],
        compiler_params=pltpu.CompilerParams(vmem_limit_bytes=1024 * 1024),
    )(*out)
    return out[0].reshape(-1), out[1], out[2], out[3].reshape(-1)


def solution(mesh):
    one, three = P(("gx", "gy")), P(None, ("gx", "gy"))
    return jax.shard_map(
        shards,
        mesh=mesh,
        in_specs=(three, one, three, three, one, one, one, one, one, one, one),
        out_specs=(one, three, three, one),
        check_vma=False,
    )
```

```python
import jax
import jax.numpy as jnp
from jax import lax
from jax.experimental import pallas as pl
from jax.experimental.pallas import tpu as pltpu
from jax.sharding import PartitionSpec as P

TILE = 128
SECTIONS = 4
SIZES = [32, 320, 32, 160, 160, 32, 320, 32]
DIRECTIONS = [(-1, -1), (-1, 0), (-1, 1), (0, -1), (0, 1), (1, -1), (1, 0), (1, 1)]
STARTS = [sum(SIZES[:d]) for d in range(8)]
BLOCKS = 16
GBLOCKS = 9
TILES = 64
COURANT = 0.3
DAMPING = 0.5
MESH = pl.DeviceIdType.MESH
F32 = jnp.float32
BF16 = jnp.bfloat16

PIECES = []
OFFSET = []
for d in range(8):
    OFFSET.append(len(PIECES))
    for k in range(STARTS[d] // TILE, (STARTS[d] + SIZES[d] - 1) // TILE + 1):
        lo = max(STARTS[d] - k * TILE, 0)
        hi = min(STARTS[d] + SIZES[d] - k * TILE, TILE)
        PIECES.append((d, k, lo, hi))
COUNT = [sum(1 for p in PIECES if p[0] == d) for d in range(8)]
NPIECE = len(PIECES)

QROWS = 40
CORNER_PIECES = sorted((lo, k, n) for n, (d, k, lo, hi) in enumerate(PIECES) if all(DIRECTIONS[d]))
CORNERS = [BLOCKS + k for lo, k, n in CORNER_PIECES]


def rkl_table(sections):
    wfirst = 4.0 / (sections * sections + sections - 2)
    bvals = [1.0 / 3.0] * 3 + [(j * j + j - 2) / (2.0 * j * (j + 1)) for j in range(3, sections + 1)]
    rows = [(1.0, 0.0, 0.0, bvals[1] * wfirst, 0.0)]
    for j in range(2, sections + 1):
        mu = (2.0 * j - 1.0) / j * bvals[j] / bvals[j - 1]
        nu = -(j - 1.0) / j * bvals[j] / bvals[j - 2]
        mut = mu * wfirst
        rows.append((mu, nu, 1.0 - mu - nu, mut, -(1.0 - bvals[j - 1]) * mut))
    return rows


def q_rows(x, live, rho, mom, bfl, psi, speed):
    inv = 1.0 / rho
    vel = [m * inv for m in mom]
    ptot = rho + 0.5 * (bfl[0] * bfl[0] + bfl[1] * bfl[1] + bfl[2] * bfl[2])
    state = [rho, *mom, *bfl, psi]
    t = {}
    for a in range(3):
        for b in range(a, 3):
            v = mom[b] * vel[a] - bfl[b] * bfl[a]
            t[a, b] = t[b, a] = v + ptot if a == b else v
    ind = {}
    for a in range(3):
        for b in range(a + 1, 3):
            ind[a, b] = vel[a] * bfl[b] - bfl[a] * vel[b]
    gsum = [x[0] * mom[0] + x[1] * mom[1] + x[2] * mom[2]]
    for k in range(3):
        gsum.append(x[0] * t[0, k] + x[1] * t[1, k] + x[2] * t[2, k])
    gsum.append(x[0] * psi - x[1] * ind[0, 1] - x[2] * ind[0, 2])
    gsum.append(x[0] * ind[0, 1] + x[1] * psi - x[2] * ind[1, 2])
    gsum.append(x[0] * ind[0, 2] + x[1] * ind[1, 2] + x[2] * psi)
    gsum.append(x[0] * bfl[0] + x[1] * bfl[1] + x[2] * bfl[2])
    return [
        live, *x, *state, *[speed * u for u in state], speed,
        t[0, 0], t[0, 1], t[0, 2], t[1, 1], t[1, 2], t[2, 2],
        ind[0, 1], ind[0, 2], ind[1, 2], *gsum,
    ]


def flux_of(q):
    m, b, psi = q[5:8], q[8:11], q[11]
    t = {(0, 0): q[21], (0, 1): q[22], (0, 2): q[23], (1, 1): q[24], (1, 2): q[25], (2, 2): q[26]}
    i01, i02, i12 = q[27:30]
    ind = [[psi, i01, i02], [-i01, psi, i12], [-i02, -i12, psi]]
    return [[m[d], *[t[min(d, k), max(d, k)] for k in range(3)], *ind[d], b[d]] for d in range(3)]


def kernel(
    pos_h, rho_h, mom_h, bfl_h, psi_h, ohm_h, amb_h, gi_h, ti_h, tj_h, cnt_h,
    rho_o, mom_o, bfl_o, psi_o,
    pos_r, rho_r, mom_r, bfl_r, psi_r, ohm_r, amb_r, gi_r, gis_r, ti_r, tj_r, cnt_r, tabv, tab,
    pk, lane_b, blk_b, pay, paysend, payrecv, ghp, qp, qt, qb, xn, xb, wst, wcor, acch, acct,
    gsrc, qdl, dsend, drecv, qdb, accd, acdt, yz, older, lz, nloc, facs,
    mxs, mxa, mxb, mxc,
    s_in, s_tab, s_pay, r_pay, s_d, r_d, s_a, r_a, s_b, r_b, s_c, r_c,
):
    ix, iy = lax.axis_index("gx"), lax.axis_index("gy")
    xx, xy = ix // 8, ix % 8

    def near(p, q):
        return ((ix + 32 + p) % 32, (iy + 16 + q) % 16)

    def dev_a(k):
        return (ix, (iy + k) % 16)

    def dev_b(k):
        return (xx * 8 + (xy + k) % 8, iy)

    def dev_c(k):
        return (((xx + k) % 4) * 8 + xy, iy)

    loads = {}
    for n, (name, src, dst) in enumerate([
        ("bfl", bfl_h, bfl_r), ("rho", rho_h, rho_r), ("pos", pos_h, pos_r), ("mom", mom_h, mom_r),
        ("psi", psi_h, psi_r), ("ohm", ohm_h, ohm_r), ("amb", amb_h, amb_r),
        ("gi", gi_h.at[pl.ds(0, 1024)], gi_r), ("gis", gi_h.at[pl.ds(1024, 64)], gis_r),
        ("ti", ti_h, ti_r), ("tj", tj_h, tj_r), ("cnt", cnt_h, cnt_r),
    ]):
        loads[name] = pltpu.make_async_copy(src, dst, s_in.at[n])
        loads[name].start()

    barrier = pltpu.get_barrier_semaphore()

    def hello(dev, n):
        def body(k, c):
            pl.semaphore_signal(barrier, inc=1, device_id=dev(k), device_id_type=MESH)
            return c

        lax.fori_loop(1, n, body, 0)

    hello(dev_a, 16)
    hello(dev_b, 8)
    hello(dev_c, 4)
    for p, q in DIRECTIONS:
        if p:
            pl.semaphore_signal(barrier, inc=1, device_id=near(p, q), device_id_type=MESH)

    def pack(n, ref):
        for j in range(BLOCKS):
            pk[pl.ds(48 * n + j, 3, stride=16), :] = ref[:, TILE * j : TILE * (j + 1)]
        return [pk[48 * n + 16 * d : 48 * n + 16 * (d + 1), :] for d in range(3)]

    def unpack(n, ref):
        for j in range(BLOCKS):
            ref[:, TILE * j : TILE * (j + 1)] = pk[pl.ds(48 * n + j, 3, stride=16), :]

    ixf = ix.astype(F32)
    iyf = iy.astype(F32)
    loads["bfl"].wait()
    loads["rho"].wait()
    rho = rho_r[...]
    bfl = pack(2, bfl_r)
    speed = jnp.sqrt(1.0 + (bfl[0] * bfl[0] + bfl[1] * bfl[1] + bfl[2] * bfl[2]) / rho)
    mxs[0] = jnp.max(speed, axis=0, keepdims=True)


    def ring(dev, n, src, dst, ss, rs):
        def one(k):
            return pltpu.make_async_remote_copy(
                src_ref=mxs.at[src], dst_ref=dst.at[k], send_sem=ss.at[k], recv_sem=rs.at[k],
                device_id=dev(k), device_id_type=MESH,
            )

        def send():
            lax.fori_loop(1, n, lambda k, c: (one(k).start(), c)[1], 0)

        def wait():
            def body(k, c):
                one(k).wait_send()
                one(k).wait_recv()
                return c

            lax.fori_loop(1, n, body, 0)
            return lax.fori_loop(1, n, lambda k, c: jnp.maximum(c, dst[k]), mxs[src])

        return send, wait

    send_a, wait_a = ring(dev_a, 16, 0, mxa, s_a, r_a)
    send_b, wait_b = ring(dev_b, 8, 1, mxb, s_b, r_b)
    send_c, wait_c = ring(dev_c, 4, 2, mxc, s_c, r_c)

    for name in ("pos", "mom", "psi", "ohm", "amb", "gi", "gis", "ti", "tj", "cnt"):
        loads[name].wait()
    x = pack(0, pos_r)
    mom = pack(1, mom_r)
    psi = psi_r[...]
    fac = amb_r[...] / (rho * jnp.sqrt(rho))
    facs[...] = fac
    live = jnp.ones_like(rho)
    zero = jnp.zeros_like(rho)
    for r, v in enumerate([*bfl, live, *mom, rho, *x, psi, speed, ohm_r[...], fac, zero]):
        pay[pl.ds(r, 16, stride=16), :] = v

    lanes = lax.broadcasted_iota(jnp.int32, (8, TILE), 1)

    def vector_of(scalar, n):
        v = jnp.zeros((8, TILE), jnp.int32)
        for m in range(n):
            v = jnp.where(lanes == m, scalar(m), v)
        return v

    for o in range(GBLOCKS):
        if o < 8:
            row = jnp.broadcast_to(gi_r[TILE * o : TILE * (o + 1)].reshape(1, TILE), (8, TILE))
        else:
            row = vector_of(lambda m: gis_r[m], 64)
        lane_b[o] = row & 127
        blk_b[o] = row >> 7

    def gathered(load):
        got = [jnp.zeros((8, TILE), F32) for _ in range(GBLOCKS)]
        for s in range(BLOCKS):
            src = load(s)
            for o in range(GBLOCKS):
                val = jnp.take_along_axis(src, lane_b[o], axis=1, mode="promise_in_bounds")
                got[o] = jnp.where(blk_b[o] == s, val, got[o])
        return got

    upper = lax.broadcasted_iota(jnp.int32, (8, TILE), 0) < 4

    def gathered4(rows):
        for r, v in enumerate(rows):
            gsrc[pl.ds(r, 8, stride=8), :] = v[:8]
            gsrc[pl.ds(4 + r, 8, stride=8), :] = v[8:]
        half = jnp.where(upper, 0, 8)
        got = [jnp.zeros((8, TILE), F32) for _ in range(GBLOCKS)]
        for o in range(GBLOCKS):
            lane, blk = lane_b[o], blk_b[o] - half
            for s in range(8):
                val = jnp.take_along_axis(gsrc[8 * s : 8 * s + 8, :], lane, axis=1, mode="promise_in_bounds")
                got[o] = jnp.where(blk == s, val, got[o])
        return [v + pltpu.roll(v, 4, 0) for v in got]

    def shifted(got):
        out = []
        for d, k, lo, hi in PIECES:
            shift = STARTS[d] - STARTS[7 - d]
            a, s = shift // TILE, shift % TILE
            if lo >= s:
                out.append(pltpu.roll(got[k - a], s, 1) if s else got[k - a])
            elif hi <= s:
                out.append(pltpu.roll(got[k - a - 1], s, 1))
            else:
                out.append(
                    jnp.where(lanes >= s, pltpu.roll(got[k - a], s, 1), pltpu.roll(got[k - a - 1], s, 1))
                )
        return out

    exists = []
    for p, q in DIRECTIONS:
        e = (ix + p >= 0) & (ix + p < 32) & (iy + q >= 0) & (iy + q < 16)
        exists.append(e)

    def combined(load, corners):
        out = []
        for k in range(1 if corners else GBLOCKS):
            tile = jnp.zeros((8, TILE), F32)
            for n, (d, kk, lo, hi) in enumerate(PIECES):
                if corners if all(DIRECTIONS[d]) and corners is not None else kk == k and not corners:
                    mask = (lanes >= lo) & (lanes < hi) & exists[d]
                    tile = jnp.where(mask, load(n), tile)
            out.append(tile)
        return out

    def copies(src, dst, ss, rs):
        out = []
        for d, (p, q) in enumerate(DIRECTIONS):
            part = pl.ds(OFFSET[d], COUNT[d])
            out.append(
                pltpu.make_async_remote_copy(
                    src_ref=src.at[part], dst_ref=dst.at[part], send_sem=ss.at[d], recv_sem=rs.at[d],
                    device_id=near(-p, -q), device_id_type=MESH,
                )
            )
        return out

    for g in range(2):
        got = gathered(lambda s, g=g: pay[16 * s + 8 * g : 16 * s + 8 * g + 8, :])
        for n, v in enumerate(shifted(got)):
            paysend[n, 8 * g : 8 * (g + 1), :] = v
    pl.semaphore_wait(barrier, 15 + 7 + 3 + 6)
    send_a()
    pay_copies = copies(paysend, payrecv, s_pay, r_pay)
    for c in pay_copies:
        c.start()

    def put_q(rows, base):
        for r, v in enumerate(rows):
            qt[pl.ds(base * QROWS + r, 16, stride=QROWS), :] = v

    qloc = q_rows([x[0] - ixf, x[1] - iyf, x[2]], live, rho, mom, bfl, psi, speed)
    for r, v in enumerate(qloc):
        qp[r] = v
    put_q([*qloc, zero, zero], 0)

    def put_x(j):
        tile = qt[pl.ds(pl.multiple_of(j * QROWS, 8), 8), :]
        tile = tile * 2.0
        xn[j] = tile
        col = jnp.transpose(tile)
        for d in range(3):
            xb[j, d] = jnp.broadcast_to(col[:, 1 + d : 2 + d], (TILE, TILE))

    def split(j):
        v = qt[pl.ds(pl.multiple_of(j * QROWS, 8), QROWS), :]
        hi = v.astype(BF16).astype(F32)
        qb[j] = jnp.concatenate([hi, v - hi], axis=0).astype(BF16)

    def prep(j, c):
        put_x(j)
        split(j)
        return c

    lax.fori_loop(0, BLOCKS, prep, 0)

    row8 = (8, TILE)
    lane = lax.broadcasted_iota(jnp.int32, row8, 1)
    used = lane < jnp.minimum(cnt_r[0], TILES)
    pair = vector_of(lambda m: ti_r[m] * 32 + tj_r[m], TILES)
    key = jnp.where(used, pair, 1024 + lane)
    keycol = jnp.broadcast_to(jnp.transpose(key)[:, 0:1], (TILE, TILE))
    keyrow = jnp.broadcast_to(key[0:1, :], (TILE, TILE))
    rank = jnp.sum(jnp.where(keycol < keyrow, 1, 0), axis=0, keepdims=True)
    rank = jnp.broadcast_to(jnp.transpose(jnp.broadcast_to(rank, row8))[:, 0:1], (TILE, TILE))
    lanes2 = lax.broadcasted_iota(jnp.int32, (TILE, TILE), 1)
    skey = jnp.sum(jnp.where(rank == lanes2, keycol, 0), axis=0, keepdims=True)
    total = jnp.sum(jnp.where(keycol < (lanes2 + 1) * 32, 1, 0), axis=0, keepdims=True)
    below = jnp.sum(jnp.where(keycol < lanes2 * 32, 1, 0), axis=0, keepdims=True)
    last = jnp.where(total > below, total - 1, TILES)
    skey = jnp.broadcast_to(skey, row8)
    valid = skey < 1024
    si = jnp.where(valid, skey >> 5, 0)
    sj = jnp.where(valid, skey & 31, 0)
    same = jnp.where((lane > 0) & (si == pltpu.roll(si, 1, 1)), 1, 0)
    sub = lax.broadcasted_iota(jnp.int32, row8, 0)
    want = (lane >> 2) * 32 + jnp.where(
        lane % 4 == 0, CORNERS[0], jnp.where(lane % 4 == 1, CORNERS[1], jnp.where(lane % 4 == 2, CORNERS[2], CORNERS[3]))
    )
    skeycol = jnp.broadcast_to(jnp.transpose(skey)[:, 0:1], (TILE, TILE))
    hit = skeycol == jnp.broadcast_to(want[0:1, :], (TILE, TILE))
    place = lax.broadcasted_iota(jnp.int32, (TILE, TILE), 0)
    corner = TILES + jnp.sum(jnp.where(hit, place - TILES, 0), axis=0, keepdims=True)
    corner = jnp.broadcast_to(corner, row8)
    tabv[...] = jnp.where(
        sub == 0, si, jnp.where(sub == 1, sj, jnp.where(sub == 2, same, jnp.where(sub == 3, last, corner)))
    )
    to_smem = pltpu.make_async_copy(tabv, tab, s_tab)
    to_smem.start()

    mxs[1] = wait_a()
    send_b()

    for c in pay_copies:
        c.wait_recv()
    for g in range(2):
        tiles = combined(lambda n, g=g: payrecv[n, 8 * g : 8 * (g + 1), :], None)
        for k, v in enumerate(tiles):
            ghp[16 * k + 8 * g : 16 * k + 8 * g + 8, :] = v
    gh = [ghp[pl.ds(r, 16, stride=16), :] for r in range(13)]
    glive = gh[3]
    grho = jnp.where(glive > 0.0, gh[7], 1.0)
    gq = q_rows(
        [glive * (gh[8] - ixf), glive * (gh[9] - iyf), gh[10]], glive, grho, gh[4:7], gh[0:3], gh[11], gh[12]
    )
    gq = [jnp.where(glive > 0.0, v, 0.0) for v in gq]
    put_q([*gq, zero, zero], BLOCKS)
    lax.fori_loop(BLOCKS, BLOCKS + GBLOCKS, prep, 0)

    def inside(index, n):
        return jnp.minimum(jnp.maximum(index, 0), n - 1)

    def fold(run, part, same):
        return part + jnp.where(same == 1, run, 0.0)

    def hydro_tile(t, run):
        i, j = inside(tab[0, t], BLOCKS), inside(tab[1, t], BLOCKS + GBLOCKS)
        a = xn[i]
        d0 = a[1:2, :] - xb[j, 0]
        d1 = a[2:3, :] - xb[j, 1]
        d2 = a[3:4, :] - xb[j, 2]
        base = jnp.maximum(1.0 - (d0 * d0 + d1 * d1 + d2 * d2), 0.0)
        w = base * base
        hi = w.astype(BF16)
        lo = (w - hi.astype(F32)).astype(BF16)
        w2 = jnp.concatenate([hi, lo], axis=0)
        wst[t] = w2
        q = qb[j]
        part = jnp.dot(jnp.concatenate([q, q], axis=1), w2, preferred_element_type=F32)
        run = fold(run, part[:QROWS] + part[QROWS:], tab[2, t])
        acch[t] = run
        return run

    def unrolled(body, first, end, start, by):
        def step(s, c):
            for u in range(by):
                c = body(s * by + u, c)
            return c

        return lax.fori_loop(first // by, end // by, step, start)

    to_smem.wait()
    acch[TILES] = jnp.zeros((QROWS, TILE), F32)
    accd[TILES] = jnp.zeros((8, TILE), F32)
    run = unrolled(hydro_tile, 0, TILES // 2, jnp.zeros((QROWS, TILE), F32), 4)
    mxs[2] = wait_b()
    send_c()
    unrolled(hydro_tile, TILES // 2, TILES, run, 4)
    wst[TILES] = jnp.zeros((2 * TILE, TILE), BF16)

    for i in range(BLOCKS):
        acct[QROWS * i : QROWS * (i + 1), :] = acch[inside(tab[3, i], TILES + 1)]

    acc = [acct[pl.ds(r, 16, stride=QROWS), :] for r in range(38)]
    qloc = [qp[r] for r in range(38)]
    fl, af = flux_of(qloc), flux_of(acc)
    n = acc[0]
    s_d_rows = [acc[1 + d] - qloc[1 + d] * n for d in range(3)]
    inv = 0.5 / (1.0 + n)
    rates = []
    for r in range(8):
        central = acc[30 + r]
        for d in range(3):
            central = central + fl[d][r] * s_d_rows[d] - qloc[1 + d] * af[d][r]
        if r == 7:
            psi_central = central
            central = 0.0
        dissip = qloc[20] * (acc[4 + r] - qloc[4 + r] * n) + acc[12 + r] - qloc[4 + r] * acc[20]
        rates.append((dissip - central) * inv)

    sub = lax.broadcasted_iota(jnp.int32, (8, TILE), 0)

    def exchange(k, rows):
        for m, v in enumerate(shifted(gathered4(rows))):
            dsend[k, m] = v
        cps = copies(dsend.at[k], drecv.at[k], s_d.at[k], r_d.at[k])
        for cp in cps:
            cp.start()
        return cps

    def dsplit(v):
        hi = v.astype(BF16).astype(F32)
        return jnp.concatenate([hi, v - hi], axis=0).astype(BF16)

    def put_local(y, eta):
        for r, v in enumerate([*y, eta, *[eta * u for u in y], zero]):
            qdl[pl.ds(r, 16, stride=8), :] = v
        for j in range(BLOCKS):
            qdb[j] = dsplit(qdl[8 * j : 8 * j + 8, :])

    def ghost_rows(v):
        eta = jnp.broadcast_to(v[3:4, :], (8, TILE))
        return dsplit(v * jnp.where(upper, 1.0, jnp.where(sub < 7, eta, 0.0)))

    cps = exchange(0, [*rates[4:7], zero])

    def corner_weights(i, c):
        for m in range(4):
            s = inside(tab[4, 4 * i + m], TILES + 1)
            for h in range(2):
                rows = pl.ds(TILE * h + 32 * m, 32)
                wcor[i, rows, :] = wst[s, rows, :]
        return c

    lax.fori_loop(0, BLOCKS, corner_weights, 0)

    chm = jnp.max(wait_c(), axis=1, keepdims=True)
    ch = jnp.broadcast_to(chm, (BLOCKS, TILE))
    dt = COURANT / ch
    dt8 = dt[:8]
    rho_o[...] = qloc[4] + dt * rates[0]
    psi_o[...] = (qloc[11] + dt * (rates[7] - ch * ch * psi_central * inv)) * jnp.exp(-DAMPING * dt * ch)
    for d in range(3):
        mom_o[16 * d : 16 * (d + 1), :] = qloc[5 + d] + dt * rates[1 + d]
        yz[d] = qloc[8 + d] + dt * rates[4 + d]
    nloc[0] = n
    nloc[1] = inv
    nloc[2] = dt
    table = rkl_table(SECTIONS)

    def eta_of(y):
        return ohm_r[...] + facs[...] * (y[0] * y[0] + y[1] * y[1] + y[2] * y[2])

    def fold_tiles(corner):
        def tile(t, run):
            q = qdb[inside(tab[1, t], BLOCKS + GBLOCKS)]
            part = jnp.dot(jnp.concatenate([q, q], axis=1), wst[t], preferred_element_type=F32)
            run = fold(run, part[:8] + part[8:], tab[2, t])
            accd[t] = run
            return run

        unrolled(tile, 0, TILES, jnp.zeros((8, TILE), F32), 16)
        q = corner()
        q2 = jnp.concatenate([q, q], axis=1)
        for i in range(BLOCKS):
            part = jnp.dot(q2, wcor[i], preferred_element_type=F32)
            acdt[8 * i : 8 * (i + 1), :] = accd[inside(tab[3, i], TILES + 1)] + (part[:8] + part[8:])
        return [acdt[pl.ds(r, 16, stride=8), :] for r in range(7)]

    def rates_of(y, eta, corner):
        acc = fold_tiles(corner)
        n, inv = nloc[0], nloc[1]
        return [(eta * (acc[d] - y[d] * n) + acc[4 + d] - y[d] * acc[3]) * inv for d in range(3)]

    y = [yz[d] for d in range(3)]
    eta = eta_of(y)
    put_local(y, eta)
    straight = [d for d in range(8) if not all(DIRECTIONS[d])]
    diagonal = [d for d in range(8) if all(DIRECTIONS[d])]

    def start_rows(g0, g1, v):
        y0 = jnp.where(sub < 3, g0 + dt8 * v, 0.0)
        sq = jnp.sum(y0 * y0, axis=0, keepdims=True)
        geta = g1[5:6, :] + g1[6:7, :] * sq
        w = jnp.where(sub == 3, jnp.broadcast_to(geta, (8, TILE)), y0)
        return ghost_rows(w + pltpu.roll(w, 4, 0))

    def payload_tile(m, g):
        return ghp[16 * m + 8 * g : 16 * m + 8 * g + 8, :]

    def keep(tile, m):
        for lo, k, n in CORNER_PIECES:
            if k == m:
                tile = jnp.where((lanes >= lo) & (lanes < lo + 32), 0.0, tile)
        return tile

    def corner_payload(g):
        tile = payload_tile(CORNER_PIECES[0][1], g)
        for lo, k, n in CORNER_PIECES[1:]:
            tile = jnp.where(lanes >= lo, payload_tile(k, g), tile)
        return tile

    for d in straight:
        cps[d].wait_recv()
    for m, v in enumerate(combined(lambda m: drecv[0, m], False)):
        qdb[BLOCKS + m] = start_rows(keep(payload_tile(m, 0), m), keep(payload_tile(m, 1), m), v)

    def corner_start():
        for d in diagonal:
            cps[d].wait_recv()
        [v] = combined(lambda m: drecv[0, m], True)
        return start_rows(corner_payload(0), corner_payload(1), v)

    rate = rates_of(y, eta, corner_start)
    mut = table[0][3]
    for d in range(3):
        lz[d] = rate[d]
        older[d] = y[d]
    y = [y[d] + mut * dt * rate[d] for d in range(3)]

    for k in range(1, SECTIONS):
        mu, nu, c0, mut, gam = table[k]
        eta = eta_of(y)
        cps += exchange(k, [*y, eta])
        put_local(y, eta)
        base = [mu * y[d] + nu * older[d] + c0 * yz[d] + gam * dt * lz[d] for d in range(3)]
        for d in range(3):
            older[d] = y[d]
        for d in straight:
            cps[8 * k + d].wait_recv()
        for m, v in enumerate(combined(lambda m, k=k: drecv[k, m], False)):
            qdb[BLOCKS + m] = ghost_rows(v)

        def corner_next(k=k):
            for d in diagonal:
                cps[8 * k + d].wait_recv()
            [v] = combined(lambda m: drecv[k, m], True)
            return ghost_rows(v)

        rate = rates_of(y, eta, corner_next)
        y = [base[d] + mut * dt * rate[d] for d in range(3)]

    for d in range(3):
        bfl_o[16 * d : 16 * (d + 1), :] = y[d]
    for c in pay_copies + cps:
        c.wait_send()


def finish(rho_p, mom_p, bfl_p, psi_p, rho_h, mom_h, bfl_h, psi_h, mom_r, bfl_r, sems):
    first = [
        pltpu.make_async_copy(rho_p, rho_h, sems.at[0]),
        pltpu.make_async_copy(psi_p, psi_h, sems.at[1]),
    ]
    for c in first:
        c.start()
    for src, dst in ((mom_p, mom_r), (bfl_p, bfl_r)):
        for j in range(BLOCKS):
            dst[:, TILE * j : TILE * (j + 1)] = src[pl.ds(j, 3, stride=16), :]
    second = [
        pltpu.make_async_copy(mom_r, mom_h, sems.at[2]),
        pltpu.make_async_copy(bfl_r, bfl_h, sems.at[3]),
    ]
    for c in second:
        c.start()
    for c in first + second:
        c.wait()


def shards(
    positions, density, momentum, field, psi, ohmic, ambipolar, ghost_index, tile_i, tile_j, tile_count
):
    def pin(v):
        return pltpu.with_memory_space_constraint(v, pltpu.HBM) if v.shape[0] != 1 else v

    def two(v):
        return v.reshape(BLOCKS, TILE)

    vmem = pl.BlockSpec(memory_space=pltpu.VMEM)
    hbm = pl.BlockSpec(memory_space=pltpu.HBM)
    V = pltpu.VMEM
    I32 = jnp.int32
    D = pltpu.SemaphoreType.DMA
    out = pl.pallas_call(
        kernel,
        out_shape=(
            jax.ShapeDtypeStruct((BLOCKS, TILE), F32),
            jax.ShapeDtypeStruct((48, TILE), F32),
            jax.ShapeDtypeStruct((48, TILE), F32),
            jax.ShapeDtypeStruct((BLOCKS, TILE), F32),
        ),
        in_specs=[hbm] * 11,
        out_specs=(vmem,) * 4,
        scratch_shapes=[
            V((3, 2048), F32), V((16, TILE), F32), V((3, 2048), F32), V((3, 2048), F32),
            V((16, TILE), F32), V((16, TILE), F32), V((16, TILE), F32),
            V((1024,), I32), pltpu.SMEM((64,), I32), pltpu.SMEM((64,), I32), pltpu.SMEM((64,), I32), pltpu.SMEM((1,), I32),
            V((8, TILE), I32), pltpu.SMEM((8, TILE), I32),
            V((144, TILE), F32),
            V((GBLOCKS, 8, TILE), jnp.int32),
            V((GBLOCKS, 8, TILE), jnp.int32),
            V((256, TILE), F32),
            V((NPIECE, 16, TILE), F32),
            V((NPIECE, 16, TILE), F32),
            V((256, TILE), F32),
            V((QROWS, BLOCKS, TILE), F32),
            V((32 * QROWS, TILE), F32),
            V((25, 2 * QROWS, TILE), BF16),
            V((25, 8, TILE), F32),
            V((25, 3, TILE, TILE), F32),
            V((TILES + 1, 2 * TILE, TILE), BF16),
            V((BLOCKS, 2 * TILE, TILE), BF16),
            V((TILES + 1, QROWS, TILE), F32),
            V((BLOCKS * QROWS, TILE), F32),
            V((64, TILE), F32),
            V((BLOCKS * 8, TILE), F32),
            V((SECTIONS, NPIECE, 8, TILE), F32),
            V((SECTIONS, NPIECE, 8, TILE), F32),
            V((25, 16, TILE), BF16),
            V((TILES + 1, 8, TILE), F32),
            V((BLOCKS * 8, TILE), F32),
            V((3, BLOCKS, TILE), F32),
            V((3, BLOCKS, TILE), F32),
            V((3, BLOCKS, TILE), F32),
            V((3, BLOCKS, TILE), F32),
            V((BLOCKS, TILE), F32),
            V((3, 1, TILE), F32),
            V((16, 1, TILE), F32),
            V((8, 1, TILE), F32),
            V((4, 1, TILE), F32),
            D((12,)), D, D((8,)), D((8,)), D((SECTIONS, 8)), D((SECTIONS, 8)),
            D((16,)), D((16,)), D((8,)), D((8,)), D((4,)), D((4,)),
        ],
        compiler_params=pltpu.CompilerParams(
            collective_id=0, has_side_effects=True, vmem_limit_bytes=48 * 1024 * 1024
        ),
    )(*map(pin, [
        positions, two(density), momentum, field, two(psi), two(ohmic), two(ambipolar),
        ghost_index, tile_i, tile_j, tile_count,
    ]))
    out = pl.pallas_call(
        finish,
        out_shape=(
            jax.ShapeDtypeStruct((BLOCKS, TILE), F32),
            jax.ShapeDtypeStruct((3, 2048), F32),
            jax.ShapeDtypeStruct((3, 2048), F32),
            jax.ShapeDtypeStruct((BLOCKS, TILE), F32),
        ),
        in_specs=[vmem] * 4,
        out_specs=(hbm,) * 4,
        scratch_shapes=[V((3, 2048), F32), V((3, 2048), F32), D((4,))],
        compiler_params=pltpu.CompilerParams(vmem_limit_bytes=1024 * 1024),
    )(*out)
    return out[0].reshape(-1), out[1], out[2], out[3].reshape(-1)


def solution(mesh):
    one, three = P(("gx", "gy")), P(None, ("gx", "gy"))
    return jax.shard_map(
        shards,
        mesh=mesh,
        in_specs=(three, one, three, three, one, one, one, one, one, one, one),
        out_specs=(one, three, three, one),
        check_vma=False,
    )
```

```python
import jax
import jax.numpy as jnp
from jax import lax
from jax.experimental import pallas as pl
from jax.experimental.pallas import tpu as pltpu
from jax.sharding import PartitionSpec as P

TILE = 128
SECTIONS = 4
SIZES = [32, 320, 32, 160, 160, 32, 320, 32]
DIRECTIONS = [(-1, -1), (-1, 0), (-1, 1), (0, -1), (0, 1), (1, -1), (1, 0), (1, 1)]
STARTS = [sum(SIZES[:d]) for d in range(8)]
BLOCKS = 16
GBLOCKS = 9
TILES = 64
COURANT = 0.3
DAMPING = 0.5
MESH = pl.DeviceIdType.MESH
F32 = jnp.float32
BF16 = jnp.bfloat16

PIECES = []
OFFSET = []
for d in range(8):
    OFFSET.append(len(PIECES))
    for k in range(STARTS[d] // TILE, (STARTS[d] + SIZES[d] - 1) // TILE + 1):
        lo = max(STARTS[d] - k * TILE, 0)
        hi = min(STARTS[d] + SIZES[d] - k * TILE, TILE)
        PIECES.append((d, k, lo, hi))
COUNT = [sum(1 for p in PIECES if p[0] == d) for d in range(8)]
NPIECE = len(PIECES)

STRAIGHT = [d for d in range(8) if not all(DIRECTIONS[d])]
DIAGONAL = [d for d in range(8) if all(DIRECTIONS[d])]

QROWS = 40
CORNER_PIECES = sorted((lo, k, n) for n, (d, k, lo, hi) in enumerate(PIECES) if all(DIRECTIONS[d]))
CORNERS = [BLOCKS + k for lo, k, n in CORNER_PIECES]


def rkl_table(sections):
    wfirst = 4.0 / (sections * sections + sections - 2)
    bvals = [1.0 / 3.0] * 3 + [(j * j + j - 2) / (2.0 * j * (j + 1)) for j in range(3, sections + 1)]
    rows = [(1.0, 0.0, 0.0, bvals[1] * wfirst, 0.0)]
    for j in range(2, sections + 1):
        mu = (2.0 * j - 1.0) / j * bvals[j] / bvals[j - 1]
        nu = -(j - 1.0) / j * bvals[j] / bvals[j - 2]
        mut = mu * wfirst
        rows.append((mu, nu, 1.0 - mu - nu, mut, -(1.0 - bvals[j - 1]) * mut))
    return rows


def q_rows(x, live, rho, mom, bfl, psi, speed):
    inv = 1.0 / rho
    vel = [m * inv for m in mom]
    ptot = rho + 0.5 * (bfl[0] * bfl[0] + bfl[1] * bfl[1] + bfl[2] * bfl[2])
    state = [rho, *mom, *bfl, psi]
    t = {}
    for a in range(3):
        for b in range(a, 3):
            v = mom[b] * vel[a] - bfl[b] * bfl[a]
            t[a, b] = t[b, a] = v + ptot if a == b else v
    ind = {}
    for a in range(3):
        for b in range(a + 1, 3):
            ind[a, b] = vel[a] * bfl[b] - bfl[a] * vel[b]
    gsum = [x[0] * mom[0] + x[1] * mom[1] + x[2] * mom[2]]
    for k in range(3):
        gsum.append(x[0] * t[0, k] + x[1] * t[1, k] + x[2] * t[2, k])
    gsum.append(x[0] * psi - x[1] * ind[0, 1] - x[2] * ind[0, 2])
    gsum.append(x[0] * ind[0, 1] + x[1] * psi - x[2] * ind[1, 2])
    gsum.append(x[0] * ind[0, 2] + x[1] * ind[1, 2] + x[2] * psi)
    gsum.append(x[0] * bfl[0] + x[1] * bfl[1] + x[2] * bfl[2])
    return [
        live, *x, *state, *[speed * u for u in state], speed,
        t[0, 0], t[0, 1], t[0, 2], t[1, 1], t[1, 2], t[2, 2],
        ind[0, 1], ind[0, 2], ind[1, 2], *gsum,
    ]


def flux_of(q):
    m, b, psi = q[5:8], q[8:11], q[11]
    t = {(0, 0): q[21], (0, 1): q[22], (0, 2): q[23], (1, 1): q[24], (1, 2): q[25], (2, 2): q[26]}
    i01, i02, i12 = q[27:30]
    ind = [[psi, i01, i02], [-i01, psi, i12], [-i02, -i12, psi]]
    return [[m[d], *[t[min(d, k), max(d, k)] for k in range(3)], *ind[d], b[d]] for d in range(3)]


def kernel(
    pos_h, rho_h, mom_h, bfl_h, psi_h, ohm_h, amb_h, gi_h, ti_h, tj_h, cnt_h,
    rho_o, mom_o, bfl_o, psi_o,
    pos_r, rho_r, mom_r, bfl_r, psi_r, ohm_r, amb_r, gi_r, gis_r, ti_r, tj_r, cnt_r, tabv, tab,
    pk, lane_b, blk_b, pay, paysend, payrecv, ghp, qp, qt, qb, xn, xb, wst, wcor, acch, acct,
    gsrc, qdl, dsend, drecv, qdb, accd, acdt, yz, older, lz, nloc, facs,
    mxs, mxa, mxb, mxc,
    s_in, s_tab, s_pay, r_pay, s_d, r_d, s_a, r_a, s_b, r_b, s_c, r_c,
):
    ix, iy = lax.axis_index("gx"), lax.axis_index("gy")
    xx, xy = ix // 8, ix % 8

    def near(p, q):
        return ((ix + 32 + p) % 32, (iy + 16 + q) % 16)

    def dev_a(k):
        return (ix, (iy + k) % 16)

    def dev_b(k):
        return (xx * 8 + (xy + k) % 8, iy)

    def dev_c(k):
        return (((xx + k) % 4) * 8 + xy, iy)

    loads = {}
    for n, (name, src, dst) in enumerate([
        ("bfl", bfl_h, bfl_r), ("rho", rho_h, rho_r), ("pos", pos_h, pos_r), ("mom", mom_h, mom_r),
        ("psi", psi_h, psi_r), ("ohm", ohm_h, ohm_r), ("amb", amb_h, amb_r),
        ("gi", gi_h.at[pl.ds(0, 1024)], gi_r), ("gis", gi_h.at[pl.ds(1024, 64)], gis_r),
        ("ti", ti_h, ti_r), ("tj", tj_h, tj_r), ("cnt", cnt_h, cnt_r),
    ]):
        loads[name] = pltpu.make_async_copy(src, dst, s_in.at[n])
        loads[name].start()

    barrier = pltpu.get_barrier_semaphore()

    def hello(dev, n):
        def body(k, c):
            pl.semaphore_signal(barrier, inc=1, device_id=dev(k), device_id_type=MESH)
            return c

        lax.fori_loop(1, n, body, 0)

    hello(dev_a, 16)
    hello(dev_b, 8)
    hello(dev_c, 4)
    for p, q in DIRECTIONS:
        if p:
            pl.semaphore_signal(barrier, inc=1, device_id=near(p, q), device_id_type=MESH)

    def pack(n, ref):
        for j in range(BLOCKS):
            pk[pl.ds(48 * n + j, 3, stride=16), :] = ref[:, TILE * j : TILE * (j + 1)]
        return [pk[48 * n + 16 * d : 48 * n + 16 * (d + 1), :] for d in range(3)]

    def unpack(n, ref):
        for j in range(BLOCKS):
            ref[:, TILE * j : TILE * (j + 1)] = pk[pl.ds(48 * n + j, 3, stride=16), :]

    ixf = ix.astype(F32)
    iyf = iy.astype(F32)
    loads["bfl"].wait()
    loads["rho"].wait()
    rho = rho_r[...]
    bfl = pack(2, bfl_r)
    speed = jnp.sqrt(1.0 + (bfl[0] * bfl[0] + bfl[1] * bfl[1] + bfl[2] * bfl[2]) / rho)
    mxs[0] = jnp.max(speed, axis=0, keepdims=True)


    def ring(dev, n, src, dst, ss, rs):
        def one(k):
            return pltpu.make_async_remote_copy(
                src_ref=mxs.at[src], dst_ref=dst.at[k], send_sem=ss.at[k], recv_sem=rs.at[k],
                device_id=dev(k), device_id_type=MESH,
            )

        def send():
            lax.fori_loop(1, n, lambda k, c: (one(k).start(), c)[1], 0)

        def wait():
            def body(k, c):
                one(k).wait_send()
                one(k).wait_recv()
                return c

            lax.fori_loop(1, n, body, 0)
            return lax.fori_loop(1, n, lambda k, c: jnp.maximum(c, dst[k]), mxs[src])

        return send, wait

    send_a, wait_a = ring(dev_a, 16, 0, mxa, s_a, r_a)
    send_b, wait_b = ring(dev_b, 8, 1, mxb, s_b, r_b)
    send_c, wait_c = ring(dev_c, 4, 2, mxc, s_c, r_c)

    pl.semaphore_wait(barrier, 15 + 7 + 3 + 6)
    send_a()
    for name in ("pos", "mom", "psi", "ohm", "amb", "gi", "gis", "ti", "tj", "cnt"):
        loads[name].wait()
    x = pack(0, pos_r)
    mom = pack(1, mom_r)
    psi = psi_r[...]
    fac = amb_r[...] / (rho * jnp.sqrt(rho))
    facs[...] = fac
    live = jnp.ones_like(rho)
    zero = jnp.zeros_like(rho)
    for r, v in enumerate([*bfl, live, *mom, rho, *x, psi, speed, ohm_r[...], fac, zero]):
        pay[pl.ds(r, 16, stride=16), :] = v

    lanes = lax.broadcasted_iota(jnp.int32, (8, TILE), 1)

    def vector_of(scalar, n):
        v = jnp.zeros((8, TILE), jnp.int32)
        for m in range(n):
            v = jnp.where(lanes == m, scalar(m), v)
        return v

    for o in range(GBLOCKS):
        if o < 8:
            row = jnp.broadcast_to(gi_r[TILE * o : TILE * (o + 1)].reshape(1, TILE), (8, TILE))
        else:
            row = vector_of(lambda m: gis_r[m], 64)
        lane_b[o] = row & 127
        blk_b[o] = row >> 7

    def gathered(load):
        got = [jnp.zeros((8, TILE), F32) for _ in range(GBLOCKS)]
        for s in range(BLOCKS):
            src = load(s)
            for o in range(GBLOCKS):
                val = jnp.take_along_axis(src, lane_b[o], axis=1, mode="promise_in_bounds")
                got[o] = jnp.where(blk_b[o] == s, val, got[o])
        return got

    upper = lax.broadcasted_iota(jnp.int32, (8, TILE), 0) < 4

    def gathered4(o):
        got = jnp.zeros((8, TILE), F32)
        lane, blk = lane_b[o], blk_b[o] - jnp.where(upper, 0, 8)
        for s in range(8):
            val = jnp.take_along_axis(gsrc[8 * s : 8 * s + 8, :], lane, axis=1, mode="promise_in_bounds")
            got = jnp.where(blk == s, val, got)
        return got + pltpu.roll(got, 4, 0)

    def shifted(piece, got):
        d, k, lo, hi = piece
        shift = STARTS[d] - STARTS[7 - d]
        a, s = shift // TILE, shift % TILE

        def turned(o):
            return pltpu.roll(got(o), s, 1) if s else got(o)

        if lo >= s:
            return turned(k - a)
        if hi <= s:
            return turned(k - a - 1)
        return jnp.where(lanes >= s, turned(k - a), turned(k - a - 1))

    exists = []
    for p, q in DIRECTIONS:
        e = (ix + p >= 0) & (ix + p < 32) & (iy + q >= 0) & (iy + q < 16)
        exists.append(e)

    def combined(load, corners):
        out = []
        for k in range(1 if corners else GBLOCKS):
            tile = jnp.zeros((8, TILE), F32)
            for n, (d, kk, lo, hi) in enumerate(PIECES):
                if corners if all(DIRECTIONS[d]) and corners is not None else kk == k and not corners:
                    mask = (lanes >= lo) & (lanes < hi) & exists[d]
                    tile = jnp.where(mask, load(n), tile)
            out.append(tile)
        return out

    def copies(src, dst, ss, rs):
        out = []
        for d, (p, q) in enumerate(DIRECTIONS):
            part = pl.ds(OFFSET[d], COUNT[d])
            out.append(
                pltpu.make_async_remote_copy(
                    src_ref=src.at[part], dst_ref=dst.at[part], send_sem=ss.at[d], recv_sem=rs.at[d],
                    device_id=near(-p, -q), device_id_type=MESH,
                )
            )
        return out

    for g in range(2):
        got = gathered(lambda s, g=g: pay[16 * s + 8 * g : 16 * s + 8 * g + 8, :])
        for n, piece in enumerate(PIECES):
            paysend[n, 8 * g : 8 * (g + 1), :] = shifted(piece, lambda o: got[o])
    pay_copies = copies(paysend, payrecv, s_pay, r_pay)
    for d in DIAGONAL + STRAIGHT:
        pay_copies[d].start()

    def put_q(rows, base):
        for r, v in enumerate(rows):
            qt[pl.ds(base * QROWS + r, 16, stride=QROWS), :] = v

    qloc = q_rows([x[0] - ixf, x[1] - iyf, x[2]], live, rho, mom, bfl, psi, speed)
    for r, v in enumerate(qloc):
        qp[r] = v
    put_q([*qloc, zero, zero], 0)

    def put_x(j):
        tile = qt[pl.ds(pl.multiple_of(j * QROWS, 8), 8), :]
        tile = tile * 2.0
        xn[j] = tile
        col = jnp.transpose(tile)
        for d in range(3):
            xb[j, d] = jnp.broadcast_to(col[:, 1 + d : 2 + d], (TILE, TILE))

    def split(j):
        v = qt[pl.ds(pl.multiple_of(j * QROWS, 8), QROWS), :]
        hi = v.astype(BF16).astype(F32)
        qb[j] = jnp.concatenate([hi, v - hi], axis=0).astype(BF16)

    def prep(first, n, by):
        def step(s, c):
            for u in range(by):
                put_x(first + s * by + u)
                split(first + s * by + u)
            return c

        lax.fori_loop(0, n // by, step, 0)

    prep(0, BLOCKS, 8)

    row8 = (8, TILE)
    lane = lax.broadcasted_iota(jnp.int32, row8, 1)
    used = lane < jnp.minimum(cnt_r[0], TILES)
    pair = vector_of(lambda m: ti_r[m] * 32 + tj_r[m], TILES)
    key = jnp.where(used, pair, 1024 + lane)
    keycol = jnp.broadcast_to(jnp.transpose(key)[:, 0:1], (TILE, TILE))
    keyrow = jnp.broadcast_to(key[0:1, :], (TILE, TILE))
    rank = jnp.sum(jnp.where(keycol < keyrow, 1, 0), axis=0, keepdims=True)
    rank = jnp.broadcast_to(jnp.transpose(jnp.broadcast_to(rank, row8))[:, 0:1], (TILE, TILE))
    lanes2 = lax.broadcasted_iota(jnp.int32, (TILE, TILE), 1)
    skey = jnp.sum(jnp.where(rank == lanes2, keycol, 0), axis=0, keepdims=True)
    total = jnp.sum(jnp.where(keycol < (lanes2 + 1) * 32, 1, 0), axis=0, keepdims=True)
    below = jnp.sum(jnp.where(keycol < lanes2 * 32, 1, 0), axis=0, keepdims=True)
    last = jnp.where(total > below, total - 1, TILES)
    skey = jnp.broadcast_to(skey, row8)
    valid = skey < 1024
    si = jnp.where(valid, skey >> 5, 0)
    sj = jnp.where(valid, skey & 31, 0)
    same = jnp.where((lane > 0) & (si == pltpu.roll(si, 1, 1)), 1, 0)
    sub = lax.broadcasted_iota(jnp.int32, row8, 0)
    want = (lane >> 2) * 32 + jnp.where(
        lane % 4 == 0, CORNERS[0], jnp.where(lane % 4 == 1, CORNERS[1], jnp.where(lane % 4 == 2, CORNERS[2], CORNERS[3]))
    )
    skeycol = jnp.broadcast_to(jnp.transpose(skey)[:, 0:1], (TILE, TILE))
    hit = skeycol == jnp.broadcast_to(want[0:1, :], (TILE, TILE))
    place = lax.broadcasted_iota(jnp.int32, (TILE, TILE), 0)
    corner = TILES + jnp.sum(jnp.where(hit, place - TILES, 0), axis=0, keepdims=True)
    corner = jnp.broadcast_to(corner, row8)
    tabv[...] = jnp.where(
        sub == 0, si, jnp.where(sub == 1, sj, jnp.where(sub == 2, same, jnp.where(sub == 3, last, corner)))
    )
    to_smem = pltpu.make_async_copy(tabv, tab, s_tab)
    to_smem.start()

    mxs[1] = wait_a()
    send_b()

    for c in pay_copies:
        c.wait_recv()
    for g in range(2):
        tiles = combined(lambda n, g=g: payrecv[n, 8 * g : 8 * (g + 1), :], None)
        for k, v in enumerate(tiles):
            ghp[16 * k + 8 * g : 16 * k + 8 * g + 8, :] = v
    gh = [ghp[pl.ds(r, 16, stride=16), :] for r in range(13)]
    glive = gh[3]
    grho = jnp.where(glive > 0.0, gh[7], 1.0)
    gq = q_rows(
        [glive * (gh[8] - ixf), glive * (gh[9] - iyf), gh[10]], glive, grho, gh[4:7], gh[0:3], gh[11], gh[12]
    )
    gq = [jnp.where(glive > 0.0, v, 0.0) for v in gq]
    put_q([*gq, zero, zero], BLOCKS)
    prep(BLOCKS, GBLOCKS, 9)

    def inside(index, n):
        return jnp.minimum(jnp.maximum(index, 0), n - 1)

    def fold(run, part, same):
        return part + jnp.where(same == 1, run, 0.0)

    def hydro_tile(t, run):
        i, j = inside(tab[0, t], BLOCKS), inside(tab[1, t], BLOCKS + GBLOCKS)
        a = xn[i]
        d0 = a[1:2, :] - xb[j, 0]
        d1 = a[2:3, :] - xb[j, 1]
        d2 = a[3:4, :] - xb[j, 2]
        base = jnp.maximum(1.0 - (d0 * d0 + d1 * d1 + d2 * d2), 0.0)
        w = base * base
        hi = w.astype(BF16)
        lo = (w - hi.astype(F32)).astype(BF16)
        w2 = jnp.concatenate([hi, lo], axis=0)
        wst[t] = w2
        q = qb[j]
        part = jnp.dot(jnp.concatenate([q, q], axis=1), w2, preferred_element_type=F32)
        run = fold(run, part[:QROWS] + part[QROWS:], tab[2, t])
        acch[t] = run
        return run

    def unrolled(body, first, end, start, by):
        def step(s, c):
            for u in range(by):
                c = body(s * by + u, c)
            return c

        return lax.fori_loop(first // by, end // by, step, start)

    to_smem.wait()
    acch[TILES] = jnp.zeros((QROWS, TILE), F32)
    accd[TILES] = jnp.zeros((8, TILE), F32)
    run = unrolled(hydro_tile, 0, TILES // 2, jnp.zeros((QROWS, TILE), F32), 16)
    mxs[2] = wait_b()
    send_c()
    unrolled(hydro_tile, TILES // 2, TILES, run, 16)
    wst[TILES] = jnp.zeros((2 * TILE, TILE), BF16)

    for i in range(BLOCKS):
        acct[QROWS * i : QROWS * (i + 1), :] = acch[inside(tab[3, i], TILES + 1)]

    acc = [acct[pl.ds(r, 16, stride=QROWS), :] for r in range(38)]
    qloc = [qp[r] for r in range(38)]
    fl, af = flux_of(qloc), flux_of(acc)
    n = acc[0]
    s_d_rows = [acc[1 + d] - qloc[1 + d] * n for d in range(3)]
    inv = 0.5 / (1.0 + n)
    rates = []
    for r in range(8):
        central = acc[30 + r]
        for d in range(3):
            central = central + fl[d][r] * s_d_rows[d] - qloc[1 + d] * af[d][r]
        if r == 7:
            psi_central = central
            central = 0.0
        dissip = qloc[20] * (acc[4 + r] - qloc[4 + r] * n) + acc[12 + r] - qloc[4 + r] * acc[20]
        rates.append((dissip - central) * inv)

    sub = lax.broadcasted_iota(jnp.int32, (8, TILE), 0)

    def exchange(k, rows):
        for r, v in enumerate(rows):
            gsrc[pl.ds(r, 8, stride=8), :] = v[:8]
            gsrc[pl.ds(4 + r, 8, stride=8), :] = v[8:]
        cps = copies(dsend.at[k], drecv.at[k], s_d.at[k], r_d.at[k])
        got = {}

        def rows_of(o):
            if o not in got:
                got[o] = gathered4(o)
            return got[o]

        for part in (DIAGONAL, STRAIGHT):
            for m, piece in enumerate(PIECES):
                if piece[0] in part:
                    dsend[k, m] = shifted(piece, rows_of)
            for d in part:
                cps[d].start()
        return cps

    def dsplit(v):
        hi = v.astype(BF16).astype(F32)
        return jnp.concatenate([hi, v - hi], axis=0).astype(BF16)

    def put_local(y, eta):
        for r, v in enumerate([*y, eta, *[eta * u for u in y], zero]):
            qdl[pl.ds(r, 16, stride=8), :] = v
        for j in range(BLOCKS):
            qdb[j] = dsplit(qdl[8 * j : 8 * j + 8, :])

    def ghost_rows(v):
        eta = jnp.broadcast_to(v[3:4, :], (8, TILE))
        return dsplit(v * jnp.where(upper, 1.0, jnp.where(sub < 7, eta, 0.0)))

    cps = exchange(0, [*rates[4:7], zero])

    def corner_weights(i, c):
        for m in range(4):
            s = inside(tab[4, 4 * i + m], TILES + 1)
            for h in range(2):
                rows = pl.ds(TILE * h + 32 * m, 32)
                wcor[i, rows, :] = wst[s, rows, :]
        return c

    lax.fori_loop(0, BLOCKS, corner_weights, 0)

    chm = jnp.max(wait_c(), axis=1, keepdims=True)
    ch = jnp.broadcast_to(chm, (BLOCKS, TILE))
    dt = COURANT / ch
    dt8 = dt[:8]
    rho_o[...] = qloc[4] + dt * rates[0]
    psi_o[...] = (qloc[11] + dt * (rates[7] - ch * ch * psi_central * inv)) * jnp.exp(-DAMPING * dt * ch)
    for d in range(3):
        mom_o[16 * d : 16 * (d + 1), :] = qloc[5 + d] + dt * rates[1 + d]
        yz[d] = qloc[8 + d] + dt * rates[4 + d]
    nloc[0] = n
    nloc[1] = inv
    nloc[2] = dt
    table = rkl_table(SECTIONS)

    def eta_of(y):
        return ohm_r[...] + facs[...] * (y[0] * y[0] + y[1] * y[1] + y[2] * y[2])

    def fold_tiles(corner):
        def tile(t, run):
            q = qdb[inside(tab[1, t], BLOCKS + GBLOCKS)]
            part = jnp.dot(jnp.concatenate([q, q], axis=1), wst[t], preferred_element_type=F32)
            run = fold(run, part[:8] + part[8:], tab[2, t])
            accd[t] = run
            return run

        unrolled(tile, 0, TILES, jnp.zeros((8, TILE), F32), 64)
        q = corner()
        q2 = jnp.concatenate([q, q], axis=1)
        for i in range(BLOCKS):
            part = jnp.dot(q2, wcor[i], preferred_element_type=F32)
            acdt[8 * i : 8 * (i + 1), :] = accd[inside(tab[3, i], TILES + 1)] + (part[:8] + part[8:])
        return [acdt[pl.ds(r, 16, stride=8), :] for r in range(7)]

    def rates_of(y, eta, corner):
        acc = fold_tiles(corner)
        n, inv = nloc[0], nloc[1]
        return [(eta * (acc[d] - y[d] * n) + acc[4 + d] - y[d] * acc[3]) * inv for d in range(3)]

    y = [yz[d] for d in range(3)]
    eta = eta_of(y)
    put_local(y, eta)
    def start_rows(g0, g1, v):
        y0 = jnp.where(sub < 3, g0 + dt8 * v, 0.0)
        sq = jnp.sum(y0 * y0, axis=0, keepdims=True)
        geta = g1[5:6, :] + g1[6:7, :] * sq
        w = jnp.where(sub == 3, jnp.broadcast_to(geta, (8, TILE)), y0)
        return ghost_rows(w + pltpu.roll(w, 4, 0))

    def payload_tile(m, g):
        return ghp[16 * m + 8 * g : 16 * m + 8 * g + 8, :]

    def keep(tile, m):
        for lo, k, n in CORNER_PIECES:
            if k == m:
                tile = jnp.where((lanes >= lo) & (lanes < lo + 32), 0.0, tile)
        return tile

    def corner_payload(g):
        tile = payload_tile(CORNER_PIECES[0][1], g)
        for lo, k, n in CORNER_PIECES[1:]:
            tile = jnp.where(lanes >= lo, payload_tile(k, g), tile)
        return tile

    for d in STRAIGHT:
        cps[d].wait_recv()
    for m, v in enumerate(combined(lambda m: drecv[0, m], False)):
        qdb[BLOCKS + m] = start_rows(keep(payload_tile(m, 0), m), keep(payload_tile(m, 1), m), v)

    def corner_start():
        for d in DIAGONAL:
            cps[d].wait_recv()
        [v] = combined(lambda m: drecv[0, m], True)
        return start_rows(corner_payload(0), corner_payload(1), v)

    rate = rates_of(y, eta, corner_start)
    mut = table[0][3]
    for d in range(3):
        lz[d] = rate[d]
        older[d] = y[d]
    y = [y[d] + mut * dt * rate[d] for d in range(3)]

    for k in range(1, SECTIONS):
        mu, nu, c0, mut, gam = table[k]
        eta = eta_of(y)
        cps += exchange(k, [*y, eta])
        put_local(y, eta)
        base = [mu * y[d] + nu * older[d] + c0 * yz[d] + gam * dt * lz[d] for d in range(3)]
        for d in range(3):
            older[d] = y[d]
        for d in STRAIGHT:
            cps[8 * k + d].wait_recv()
        for m, v in enumerate(combined(lambda m, k=k: drecv[k, m], False)):
            qdb[BLOCKS + m] = ghost_rows(v)

        def corner_next(k=k):
            for d in DIAGONAL:
                cps[8 * k + d].wait_recv()
            [v] = combined(lambda m: drecv[k, m], True)
            return ghost_rows(v)

        rate = rates_of(y, eta, corner_next)
        y = [base[d] + mut * dt * rate[d] for d in range(3)]

    for d in range(3):
        bfl_o[16 * d : 16 * (d + 1), :] = y[d]
    for c in pay_copies + cps:
        c.wait_send()


def finish(rho_p, mom_p, bfl_p, psi_p, rho_h, mom_h, bfl_h, psi_h, mom_r, bfl_r, sems):
    first = [
        pltpu.make_async_copy(rho_p, rho_h, sems.at[0]),
        pltpu.make_async_copy(psi_p, psi_h, sems.at[1]),
    ]
    for c in first:
        c.start()
    for src, dst in ((mom_p, mom_r), (bfl_p, bfl_r)):
        for j in range(BLOCKS):
            dst[:, TILE * j : TILE * (j + 1)] = src[pl.ds(j, 3, stride=16), :]
    second = [
        pltpu.make_async_copy(mom_r, mom_h, sems.at[2]),
        pltpu.make_async_copy(bfl_r, bfl_h, sems.at[3]),
    ]
    for c in second:
        c.start()
    for c in first + second:
        c.wait()


def shards(
    positions, density, momentum, field, psi, ohmic, ambipolar, ghost_index, tile_i, tile_j, tile_count
):
    def pin(v):
        return pltpu.with_memory_space_constraint(v, pltpu.HBM) if v.shape[0] != 1 else v

    def two(v):
        return v.reshape(BLOCKS, TILE)

    vmem = pl.BlockSpec(memory_space=pltpu.VMEM)
    hbm = pl.BlockSpec(memory_space=pltpu.HBM)
    V = pltpu.VMEM
    I32 = jnp.int32
    D = pltpu.SemaphoreType.DMA
    out = pl.pallas_call(
        kernel,
        out_shape=(
            jax.ShapeDtypeStruct((BLOCKS, TILE), F32),
            jax.ShapeDtypeStruct((48, TILE), F32),
            jax.ShapeDtypeStruct((48, TILE), F32),
            jax.ShapeDtypeStruct((BLOCKS, TILE), F32),
        ),
        in_specs=[hbm] * 11,
        out_specs=(vmem,) * 4,
        scratch_shapes=[
            V((3, 2048), F32), V((16, TILE), F32), V((3, 2048), F32), V((3, 2048), F32),
            V((16, TILE), F32), V((16, TILE), F32), V((16, TILE), F32),
            V((1024,), I32), pltpu.SMEM((64,), I32), pltpu.SMEM((64,), I32), pltpu.SMEM((64,), I32), pltpu.SMEM((1,), I32),
            V((8, TILE), I32), pltpu.SMEM((8, TILE), I32),
            V((144, TILE), F32),
            V((GBLOCKS, 8, TILE), jnp.int32),
            V((GBLOCKS, 8, TILE), jnp.int32),
            V((256, TILE), F32),
            V((NPIECE, 16, TILE), F32),
            V((NPIECE, 16, TILE), F32),
            V((256, TILE), F32),
            V((QROWS, BLOCKS, TILE), F32),
            V((32 * QROWS, TILE), F32),
            V((25, 2 * QROWS, TILE), BF16),
            V((25, 8, TILE), F32),
            V((25, 3, TILE, TILE), F32),
            V((TILES + 1, 2 * TILE, TILE), BF16),
            V((BLOCKS, 2 * TILE, TILE), BF16),
            V((TILES + 1, QROWS, TILE), F32),
            V((BLOCKS * QROWS, TILE), F32),
            V((64, TILE), F32),
            V((BLOCKS * 8, TILE), F32),
            V((SECTIONS, NPIECE, 8, TILE), F32),
            V((SECTIONS, NPIECE, 8, TILE), F32),
            V((25, 16, TILE), BF16),
            V((TILES + 1, 8, TILE), F32),
            V((BLOCKS * 8, TILE), F32),
            V((3, BLOCKS, TILE), F32),
            V((3, BLOCKS, TILE), F32),
            V((3, BLOCKS, TILE), F32),
            V((3, BLOCKS, TILE), F32),
            V((BLOCKS, TILE), F32),
            V((3, 1, TILE), F32),
            V((16, 1, TILE), F32),
            V((8, 1, TILE), F32),
            V((4, 1, TILE), F32),
            D((12,)), D, D((8,)), D((8,)), D((SECTIONS, 8)), D((SECTIONS, 8)),
            D((16,)), D((16,)), D((8,)), D((8,)), D((4,)), D((4,)),
        ],
        compiler_params=pltpu.CompilerParams(
            collective_id=0, has_side_effects=True, vmem_limit_bytes=48 * 1024 * 1024
        ),
    )(*map(pin, [
        positions, two(density), momentum, field, two(psi), two(ohmic), two(ambipolar),
        ghost_index, tile_i, tile_j, tile_count,
    ]))
    out = pl.pallas_call(
        finish,
        out_shape=(
            jax.ShapeDtypeStruct((BLOCKS, TILE), F32),
            jax.ShapeDtypeStruct((3, 2048), F32),
            jax.ShapeDtypeStruct((3, 2048), F32),
            jax.ShapeDtypeStruct((BLOCKS, TILE), F32),
        ),
        in_specs=[vmem] * 4,
        out_specs=(hbm,) * 4,
        scratch_shapes=[V((3, 2048), F32), V((3, 2048), F32), D((4,))],
        compiler_params=pltpu.CompilerParams(vmem_limit_bytes=1024 * 1024),
    )(*out)
    return out[0].reshape(-1), out[1], out[2], out[3].reshape(-1)


def solution(mesh):
    one, three = P(("gx", "gy")), P(None, ("gx", "gy"))
    return jax.shard_map(
        shards,
        mesh=mesh,
        in_specs=(three, one, three, three, one, one, one, one, one, one, one),
        out_specs=(one, three, three, one),
        check_vma=False,
    )
```

```python
import jax
import jax.numpy as jnp
from jax import lax
from jax.experimental import pallas as pl
from jax.experimental.pallas import tpu as pltpu
from jax.sharding import PartitionSpec as P

TILE = 128
SECTIONS = 4
SIZES = [32, 320, 32, 160, 160, 32, 320, 32]
DIRECTIONS = [(-1, -1), (-1, 0), (-1, 1), (0, -1), (0, 1), (1, -1), (1, 0), (1, 1)]
STARTS = [sum(SIZES[:d]) for d in range(8)]
BLOCKS = 16
GBLOCKS = 9
TILES = 64
COURANT = 0.3
DAMPING = 0.5
MESH = pl.DeviceIdType.MESH
F32 = jnp.float32
BF16 = jnp.bfloat16

PIECES = []
OFFSET = []
for d in range(8):
    OFFSET.append(len(PIECES))
    for k in range(STARTS[d] // TILE, (STARTS[d] + SIZES[d] - 1) // TILE + 1):
        lo = max(STARTS[d] - k * TILE, 0)
        hi = min(STARTS[d] + SIZES[d] - k * TILE, TILE)
        PIECES.append((d, k, lo, hi))
COUNT = [sum(1 for p in PIECES if p[0] == d) for d in range(8)]
NPIECE = len(PIECES)

STRAIGHT = [d for d in range(8) if not all(DIRECTIONS[d])]
DIAGONAL = [d for d in range(8) if all(DIRECTIONS[d])]

QROWS = 40
CORNER_PIECES = sorted((lo, k, n) for n, (d, k, lo, hi) in enumerate(PIECES) if all(DIRECTIONS[d]))
CORNERS = [BLOCKS + k for lo, k, n in CORNER_PIECES]


def rkl_table(sections):
    wfirst = 4.0 / (sections * sections + sections - 2)
    bvals = [1.0 / 3.0] * 3 + [(j * j + j - 2) / (2.0 * j * (j + 1)) for j in range(3, sections + 1)]
    rows = [(1.0, 0.0, 0.0, bvals[1] * wfirst, 0.0)]
    for j in range(2, sections + 1):
        mu = (2.0 * j - 1.0) / j * bvals[j] / bvals[j - 1]
        nu = -(j - 1.0) / j * bvals[j] / bvals[j - 2]
        mut = mu * wfirst
        rows.append((mu, nu, 1.0 - mu - nu, mut, -(1.0 - bvals[j - 1]) * mut))
    return rows


def q_rows(x, live, rho, mom, bfl, psi, speed):
    inv = 1.0 / rho
    vel = [m * inv for m in mom]
    ptot = rho + 0.5 * (bfl[0] * bfl[0] + bfl[1] * bfl[1] + bfl[2] * bfl[2])
    state = [rho, *mom, *bfl, psi]
    t = {}
    for a in range(3):
        for b in range(a, 3):
            v = mom[b] * vel[a] - bfl[b] * bfl[a]
            t[a, b] = t[b, a] = v + ptot if a == b else v
    ind = {}
    for a in range(3):
        for b in range(a + 1, 3):
            ind[a, b] = vel[a] * bfl[b] - bfl[a] * vel[b]
    gsum = [x[0] * mom[0] + x[1] * mom[1] + x[2] * mom[2]]
    for k in range(3):
        gsum.append(x[0] * t[0, k] + x[1] * t[1, k] + x[2] * t[2, k])
    gsum.append(x[0] * psi - x[1] * ind[0, 1] - x[2] * ind[0, 2])
    gsum.append(x[0] * ind[0, 1] + x[1] * psi - x[2] * ind[1, 2])
    gsum.append(x[0] * ind[0, 2] + x[1] * ind[1, 2] + x[2] * psi)
    gsum.append(x[0] * bfl[0] + x[1] * bfl[1] + x[2] * bfl[2])
    return [
        live, *x, *state, *[speed * u for u in state], speed,
        t[0, 0], t[0, 1], t[0, 2], t[1, 1], t[1, 2], t[2, 2],
        ind[0, 1], ind[0, 2], ind[1, 2], *gsum,
    ]


def flux_of(q):
    m, b, psi = q[5:8], q[8:11], q[11]
    t = {(0, 0): q[21], (0, 1): q[22], (0, 2): q[23], (1, 1): q[24], (1, 2): q[25], (2, 2): q[26]}
    i01, i02, i12 = q[27:30]
    ind = [[psi, i01, i02], [-i01, psi, i12], [-i02, -i12, psi]]
    return [[m[d], *[t[min(d, k), max(d, k)] for k in range(3)], *ind[d], b[d]] for d in range(3)]


def kernel(
    pos_h, rho_h, mom_h, bfl_h, psi_h, ohm_h, amb_h, gi_h, ti_h, tj_h, cnt_h,
    rho_o, mom_o, bfl_o, psi_o,
    pos_r, rho_r, mom_r, bfl_r, psi_r, ohm_r, amb_r, gi_r, gis_r, ti_r, tj_r, cnt_r, tabv, tab,
    pk, lane_b, blk_b, pay, paysend, payrecv, ghp, qp, qt, qb, xn, xb, wst, wcor, acch, acct,
    gsrc, qdl, dsend, drecv, qdb, accd, acdt, yz, older, lz, nloc, facs,
    mxs, mxa, mxb, mxc,
    s_in, s_tab, s_pay, r_pay, s_d, r_d, s_a, r_a, s_b, r_b, s_c, r_c,
):
    ix, iy = lax.axis_index("gx"), lax.axis_index("gy")
    xx, xy = ix // 8, ix % 8

    def near(p, q):
        return ((ix + 32 + p) % 32, (iy + 16 + q) % 16)

    def dev_a(k):
        return (ix, (iy + k) % 16)

    def dev_b(k):
        return (xx * 8 + (xy + k) % 8, iy)

    def dev_c(k):
        return (((xx + k) % 4) * 8 + xy, iy)

    loads = {}
    for n, (name, src, dst) in enumerate([
        ("bfl", bfl_h, bfl_r), ("rho", rho_h, rho_r), ("pos", pos_h, pos_r), ("mom", mom_h, mom_r),
        ("psi", psi_h, psi_r), ("ohm", ohm_h, ohm_r), ("amb", amb_h, amb_r),
        ("gi", gi_h.at[pl.ds(0, 1024)], gi_r), ("gis", gi_h.at[pl.ds(1024, 64)], gis_r),
        ("ti", ti_h, ti_r), ("tj", tj_h, tj_r), ("cnt", cnt_h, cnt_r),
    ]):
        loads[name] = pltpu.make_async_copy(src, dst, s_in.at[n])
        loads[name].start()

    barrier = pltpu.get_barrier_semaphore()

    def hello(dev, n):
        def body(k, c):
            pl.semaphore_signal(barrier, inc=1, device_id=dev(k), device_id_type=MESH)
            return c

        lax.fori_loop(1, n, body, 0)

    hello(dev_a, 16)
    hello(dev_b, 8)
    hello(dev_c, 4)
    for p, q in DIRECTIONS:
        if p:
            pl.semaphore_signal(barrier, inc=1, device_id=near(p, q), device_id_type=MESH)

    def pack(n, ref):
        for j in range(BLOCKS):
            pk[pl.ds(48 * n + j, 3, stride=16), :] = ref[:, TILE * j : TILE * (j + 1)]
        return [pk[48 * n + 16 * d : 48 * n + 16 * (d + 1), :] for d in range(3)]

    def unpack(n, ref):
        for j in range(BLOCKS):
            ref[:, TILE * j : TILE * (j + 1)] = pk[pl.ds(48 * n + j, 3, stride=16), :]

    ixf = ix.astype(F32)
    iyf = iy.astype(F32)
    loads["bfl"].wait()
    loads["rho"].wait()
    rho = rho_r[...]
    bfl = pack(2, bfl_r)
    speed = jnp.sqrt(1.0 + (bfl[0] * bfl[0] + bfl[1] * bfl[1] + bfl[2] * bfl[2]) / rho)
    mxs[0] = jnp.max(speed, axis=0, keepdims=True)


    def ring(dev, n, src, dst, ss, rs):
        def one(k):
            return pltpu.make_async_remote_copy(
                src_ref=mxs.at[src], dst_ref=dst.at[k], send_sem=ss.at[k], recv_sem=rs.at[k],
                device_id=dev(k), device_id_type=MESH,
            )

        def send():
            lax.fori_loop(1, n, lambda k, c: (one(k).start(), c)[1], 0)

        def wait():
            def body(k, c):
                one(k).wait_send()
                one(k).wait_recv()
                return c

            lax.fori_loop(1, n, body, 0)
            return lax.fori_loop(1, n, lambda k, c: jnp.maximum(c, dst[k]), mxs[src])

        return send, wait

    send_a, wait_a = ring(dev_a, 16, 0, mxa, s_a, r_a)
    send_b, wait_b = ring(dev_b, 8, 1, mxb, s_b, r_b)
    send_c, wait_c = ring(dev_c, 4, 2, mxc, s_c, r_c)

    pl.semaphore_wait(barrier, 15 + 7 + 3 + 6)
    send_a()
    for name in ("pos", "mom", "psi", "ohm", "amb", "gi", "gis", "ti", "tj", "cnt"):
        loads[name].wait()
    x = pack(0, pos_r)
    mom = pack(1, mom_r)
    psi = psi_r[...]
    fac = amb_r[...] / (rho * jnp.sqrt(rho))
    facs[...] = fac
    live = jnp.ones_like(rho)
    zero = jnp.zeros_like(rho)
    for r, v in enumerate([*bfl, live, *mom, rho, *x, psi, speed, ohm_r[...], fac, zero]):
        pay[pl.ds(r, 16, stride=16), :] = v

    lanes = lax.broadcasted_iota(jnp.int32, (8, TILE), 1)

    def vector_of(scalar, n):
        v = jnp.zeros((8, TILE), jnp.int32)
        for m in range(n):
            v = jnp.where(lanes == m, scalar(m), v)
        return v

    for o in range(GBLOCKS):
        if o < 8:
            row = jnp.broadcast_to(gi_r[TILE * o : TILE * (o + 1)].reshape(1, TILE), (8, TILE))
        else:
            row = vector_of(lambda m: gis_r[m], 64)
        lane_b[o] = row & 127
        blk_b[o] = row >> 7

    def gathered(load):
        got = [jnp.zeros((8, TILE), F32) for _ in range(GBLOCKS)]
        for s in range(BLOCKS):
            src = load(s)
            for o in range(GBLOCKS):
                val = jnp.take_along_axis(src, lane_b[o], axis=1, mode="promise_in_bounds")
                got[o] = jnp.where(blk_b[o] == s, val, got[o])
        return got

    upper = lax.broadcasted_iota(jnp.int32, (8, TILE), 0) < 4

    def gathered4(o):
        got = jnp.zeros((8, TILE), F32)
        lane, blk = lane_b[o], blk_b[o] - jnp.where(upper, 0, 8)
        for s in range(8):
            val = jnp.take_along_axis(gsrc[8 * s : 8 * s + 8, :], lane, axis=1, mode="promise_in_bounds")
            got = jnp.where(blk == s, val, got)
        return got + pltpu.roll(got, 4, 0)

    def shifted(piece, got):
        d, k, lo, hi = piece
        shift = STARTS[d] - STARTS[7 - d]
        a, s = shift // TILE, shift % TILE

        def turned(o):
            return pltpu.roll(got(o), s, 1) if s else got(o)

        if lo >= s:
            return turned(k - a)
        if hi <= s:
            return turned(k - a - 1)
        return jnp.where(lanes >= s, turned(k - a), turned(k - a - 1))

    exists = []
    for p, q in DIRECTIONS:
        e = (ix + p >= 0) & (ix + p < 32) & (iy + q >= 0) & (iy + q < 16)
        exists.append(e)

    def combined(load, corners):
        out = []
        for k in range(1 if corners else GBLOCKS):
            tile = jnp.zeros((8, TILE), F32)
            for n, (d, kk, lo, hi) in enumerate(PIECES):
                if corners if all(DIRECTIONS[d]) and corners is not None else kk == k and not corners:
                    mask = (lanes >= lo) & (lanes < hi) & exists[d]
                    tile = jnp.where(mask, load(n), tile)
            out.append(tile)
        return out

    def copies(src, dst, ss, rs):
        out = []
        for d, (p, q) in enumerate(DIRECTIONS):
            part = pl.ds(OFFSET[d], COUNT[d])
            out.append(
                pltpu.make_async_remote_copy(
                    src_ref=src.at[part], dst_ref=dst.at[part], send_sem=ss.at[d], recv_sem=rs.at[d],
                    device_id=near(-p, -q), device_id_type=MESH,
                )
            )
        return out

    for g in range(2):
        got = gathered(lambda s, g=g: pay[16 * s + 8 * g : 16 * s + 8 * g + 8, :])
        for n, piece in enumerate(PIECES):
            paysend[n, 8 * g : 8 * (g + 1), :] = shifted(piece, lambda o: got[o])
    pay_copies = copies(paysend, payrecv, s_pay, r_pay)
    for d in DIAGONAL + STRAIGHT:
        pay_copies[d].start()

    def put_q(rows, base):
        for r, v in enumerate(rows):
            qt[pl.ds(base * QROWS + r, 16, stride=QROWS), :] = v

    qloc = q_rows([x[0] - ixf, x[1] - iyf, x[2]], live, rho, mom, bfl, psi, speed)
    for r, v in enumerate(qloc):
        qp[r] = v
    put_q([*qloc, zero, zero], 0)

    def put_x(j):
        tile = qt[pl.ds(pl.multiple_of(j * QROWS, 8), 8), :]
        tile = tile * 2.0
        xn[j] = tile
        col = jnp.transpose(tile)
        for d in range(3):
            xb[j, d] = jnp.broadcast_to(col[:, 1 + d : 2 + d], (TILE, TILE))

    def split(j):
        v = qt[pl.ds(pl.multiple_of(j * QROWS, 8), QROWS), :]
        hi = v.astype(BF16).astype(F32)
        qb[j] = jnp.concatenate([hi, v - hi], axis=0).astype(BF16)

    def prep(first, n, by):
        def step(s, c):
            for u in range(by):
                put_x(first + s * by + u)
                split(first + s * by + u)
            return c

        lax.fori_loop(0, n // by, step, 0)

    prep(0, BLOCKS, 8)

    row8 = (8, TILE)
    lane = lax.broadcasted_iota(jnp.int32, row8, 1)
    used = lane < jnp.minimum(cnt_r[0], TILES)
    pair = vector_of(lambda m: ti_r[m] * 32 + tj_r[m], TILES)
    key = jnp.where(used, pair, 1024 + lane)
    keycol = jnp.broadcast_to(jnp.transpose(key)[:, 0:1], (TILE, TILE))
    keyrow = jnp.broadcast_to(key[0:1, :], (TILE, TILE))
    rank = jnp.sum(jnp.where(keycol < keyrow, 1, 0), axis=0, keepdims=True)
    rank = jnp.broadcast_to(jnp.transpose(jnp.broadcast_to(rank, row8))[:, 0:1], (TILE, TILE))
    lanes2 = lax.broadcasted_iota(jnp.int32, (TILE, TILE), 1)
    skey = jnp.sum(jnp.where(rank == lanes2, keycol, 0), axis=0, keepdims=True)
    total = jnp.sum(jnp.where(keycol < (lanes2 + 1) * 32, 1, 0), axis=0, keepdims=True)
    below = jnp.sum(jnp.where(keycol < lanes2 * 32, 1, 0), axis=0, keepdims=True)
    last = jnp.where(total > below, total - 1, TILES)
    skey = jnp.broadcast_to(skey, row8)
    valid = skey < 1024
    si = jnp.where(valid, skey >> 5, 0)
    sj = jnp.where(valid, skey & 31, 0)
    same = jnp.where((lane > 0) & (si == pltpu.roll(si, 1, 1)), 1, 0)
    sub = lax.broadcasted_iota(jnp.int32, row8, 0)
    want = (lane >> 2) * 32 + jnp.where(
        lane % 4 == 0, CORNERS[0], jnp.where(lane % 4 == 1, CORNERS[1], jnp.where(lane % 4 == 2, CORNERS[2], CORNERS[3]))
    )
    skeycol = jnp.broadcast_to(jnp.transpose(skey)[:, 0:1], (TILE, TILE))
    hit = skeycol == jnp.broadcast_to(want[0:1, :], (TILE, TILE))
    place = lax.broadcasted_iota(jnp.int32, (TILE, TILE), 0)
    corner = TILES + jnp.sum(jnp.where(hit, place - TILES, 0), axis=0, keepdims=True)
    corner = jnp.broadcast_to(corner, row8)
    tabv[...] = jnp.where(
        sub == 0, si, jnp.where(sub == 1, sj, jnp.where(sub == 2, same, jnp.where(sub == 3, last, corner)))
    )
    to_smem = pltpu.make_async_copy(tabv, tab, s_tab)
    to_smem.start()

    mxs[1] = wait_a()
    send_b()

    for c in pay_copies:
        c.wait_recv()
    for g in range(2):
        tiles = combined(lambda n, g=g: payrecv[n, 8 * g : 8 * (g + 1), :], None)
        for k, v in enumerate(tiles):
            ghp[16 * k + 8 * g : 16 * k + 8 * g + 8, :] = v
    gh = [ghp[pl.ds(r, 16, stride=16), :] for r in range(13)]
    glive = gh[3]
    grho = jnp.where(glive > 0.0, gh[7], 1.0)
    gq = q_rows(
        [glive * (gh[8] - ixf), glive * (gh[9] - iyf), gh[10]], glive, grho, gh[4:7], gh[0:3], gh[11], gh[12]
    )
    gq = [jnp.where(glive > 0.0, v, 0.0) for v in gq]
    put_q([*gq, zero, zero], BLOCKS)
    prep(BLOCKS, GBLOCKS, 9)

    def inside(index, n):
        return jnp.minimum(jnp.maximum(index, 0), n - 1)

    def fold(run, part, same):
        return part + jnp.where(same == 1, run, 0.0)

    def hydro_tile(t, run):
        i, j = inside(tab[0, t], BLOCKS), inside(tab[1, t], BLOCKS + GBLOCKS)
        a = xn[i]
        d0 = a[1:2, :] - xb[j, 0]
        d1 = a[2:3, :] - xb[j, 1]
        d2 = a[3:4, :] - xb[j, 2]
        base = jnp.maximum(1.0 - (d0 * d0 + d1 * d1 + d2 * d2), 0.0)
        w = base * base
        hi = w.astype(BF16)
        lo = (w - hi.astype(F32)).astype(BF16)
        w2 = jnp.concatenate([hi, lo], axis=0)
        wst[t] = w2
        q = qb[j]
        part = jnp.dot(jnp.concatenate([q, q], axis=1), w2, preferred_element_type=F32)
        run = fold(run, part[:QROWS] + part[QROWS:], tab[2, t])
        acch[t] = run
        return run

    def unrolled(body, first, end, start, by):
        def step(s, c):
            for u in range(by):
                c = body(s * by + u, c)
            return c

        return lax.fori_loop(first // by, end // by, step, start)

    to_smem.wait()
    acch[TILES] = jnp.zeros((QROWS, TILE), F32)
    accd[TILES] = jnp.zeros((8, TILE), F32)
    run = unrolled(hydro_tile, 0, TILES // 2, jnp.zeros((QROWS, TILE), F32), 32)
    mxs[2] = wait_b()
    send_c()
    unrolled(hydro_tile, TILES // 2, TILES, run, 32)
    wst[TILES] = jnp.zeros((2 * TILE, TILE), BF16)

    for i in range(BLOCKS):
        acct[QROWS * i : QROWS * (i + 1), :] = acch[inside(tab[3, i], TILES + 1)]

    acc = [acct[pl.ds(r, 16, stride=QROWS), :] for r in range(38)]
    qloc = [qp[r] for r in range(38)]
    fl, af = flux_of(qloc), flux_of(acc)
    n = acc[0]
    s_d_rows = [acc[1 + d] - qloc[1 + d] * n for d in range(3)]
    inv = 0.5 / (1.0 + n)
    rates = []
    for r in range(8):
        central = acc[30 + r]
        for d in range(3):
            central = central + fl[d][r] * s_d_rows[d] - qloc[1 + d] * af[d][r]
        if r == 7:
            psi_central = central
            central = 0.0
        dissip = qloc[20] * (acc[4 + r] - qloc[4 + r] * n) + acc[12 + r] - qloc[4 + r] * acc[20]
        rates.append((dissip - central) * inv)

    sub = lax.broadcasted_iota(jnp.int32, (8, TILE), 0)

    def exchange(k, rows):
        for r, v in enumerate(rows):
            gsrc[pl.ds(r, 8, stride=8), :] = v[:8]
            gsrc[pl.ds(4 + r, 8, stride=8), :] = v[8:]
        cps = copies(dsend.at[k], drecv.at[k], s_d.at[k], r_d.at[k])
        got = {}

        def rows_of(o):
            if o not in got:
                got[o] = gathered4(o)
            return got[o]

        for part in (DIAGONAL, STRAIGHT):
            for m, piece in enumerate(PIECES):
                if piece[0] in part:
                    dsend[k, m] = shifted(piece, rows_of)
            for d in part:
                cps[d].start()
        return cps

    def dsplit(v):
        hi = v.astype(BF16).astype(F32)
        return jnp.concatenate([hi, v - hi], axis=0).astype(BF16)

    def put_local(y, eta):
        for r, v in enumerate([*y, eta, *[eta * u for u in y], zero]):
            qdl[pl.ds(r, 16, stride=8), :] = v
        for j in range(BLOCKS):
            qdb[j] = dsplit(qdl[8 * j : 8 * j + 8, :])

    def ghost_rows(v):
        eta = jnp.broadcast_to(v[3:4, :], (8, TILE))
        return dsplit(v * jnp.where(upper, 1.0, jnp.where(sub < 7, eta, 0.0)))

    cps = exchange(0, [*rates[4:7], zero])

    def corner_weights(i, c):
        for m in range(4):
            s = inside(tab[4, 4 * i + m], TILES + 1)
            for h in range(2):
                rows = pl.ds(TILE * h + 32 * m, 32)
                wcor[i, rows, :] = wst[s, rows, :]
        return c

    lax.fori_loop(0, BLOCKS, corner_weights, 0)

    chm = jnp.max(wait_c(), axis=1, keepdims=True)
    ch = jnp.broadcast_to(chm, (BLOCKS, TILE))
    dt = COURANT / ch
    dt8 = dt[:8]
    rho_o[...] = qloc[4] + dt * rates[0]
    psi_o[...] = (qloc[11] + dt * (rates[7] - ch * ch * psi_central * inv)) * jnp.exp(-DAMPING * dt * ch)
    for d in range(3):
        mom_o[16 * d : 16 * (d + 1), :] = qloc[5 + d] + dt * rates[1 + d]
        yz[d] = qloc[8 + d] + dt * rates[4 + d]
    nloc[0] = n
    nloc[1] = inv
    nloc[2] = dt
    table = rkl_table(SECTIONS)

    def eta_of(y):
        return ohm_r[...] + facs[...] * (y[0] * y[0] + y[1] * y[1] + y[2] * y[2])

    def fold_tiles(corner):
        def tile(t, run):
            q = qdb[inside(tab[1, t], BLOCKS + GBLOCKS)]
            part = jnp.dot(jnp.concatenate([q, q], axis=1), wst[t], preferred_element_type=F32)
            run = fold(run, part[:8] + part[8:], tab[2, t])
            accd[t] = run
            return run

        unrolled(tile, 0, TILES, jnp.zeros((8, TILE), F32), 64)
        q = corner()
        q2 = jnp.concatenate([q, q], axis=1)
        for i in range(BLOCKS):
            part = jnp.dot(q2, wcor[i], preferred_element_type=F32)
            acdt[8 * i : 8 * (i + 1), :] = accd[inside(tab[3, i], TILES + 1)] + (part[:8] + part[8:])
        return [acdt[pl.ds(r, 16, stride=8), :] for r in range(7)]

    def rates_of(y, eta, corner):
        acc = fold_tiles(corner)
        n, inv = nloc[0], nloc[1]
        return [(eta * (acc[d] - y[d] * n) + acc[4 + d] - y[d] * acc[3]) * inv for d in range(3)]

    y = [yz[d] for d in range(3)]
    eta = eta_of(y)
    put_local(y, eta)
    def start_rows(g0, g1, v):
        y0 = jnp.where(sub < 3, g0 + dt8 * v, 0.0)
        sq = jnp.sum(y0 * y0, axis=0, keepdims=True)
        geta = g1[5:6, :] + g1[6:7, :] * sq
        w = jnp.where(sub == 3, jnp.broadcast_to(geta, (8, TILE)), y0)
        return ghost_rows(w + pltpu.roll(w, 4, 0))

    def payload_tile(m, g):
        return ghp[16 * m + 8 * g : 16 * m + 8 * g + 8, :]

    def keep(tile, m):
        for lo, k, n in CORNER_PIECES:
            if k == m:
                tile = jnp.where((lanes >= lo) & (lanes < lo + 32), 0.0, tile)
        return tile

    def corner_payload(g):
        tile = payload_tile(CORNER_PIECES[0][1], g)
        for lo, k, n in CORNER_PIECES[1:]:
            tile = jnp.where(lanes >= lo, payload_tile(k, g), tile)
        return tile

    for d in STRAIGHT:
        cps[d].wait_recv()
    for m, v in enumerate(combined(lambda m: drecv[0, m], False)):
        qdb[BLOCKS + m] = start_rows(keep(payload_tile(m, 0), m), keep(payload_tile(m, 1), m), v)

    def corner_start():
        for d in DIAGONAL:
            cps[d].wait_recv()
        [v] = combined(lambda m: drecv[0, m], True)
        return start_rows(corner_payload(0), corner_payload(1), v)

    rate = rates_of(y, eta, corner_start)
    mut = table[0][3]
    for d in range(3):
        lz[d] = rate[d]
        older[d] = y[d]
    y = [y[d] + mut * dt * rate[d] for d in range(3)]

    for k in range(1, SECTIONS):
        mu, nu, c0, mut, gam = table[k]
        eta = eta_of(y)
        cps += exchange(k, [*y, eta])
        put_local(y, eta)
        base = [mu * y[d] + nu * older[d] + c0 * yz[d] + gam * dt * lz[d] for d in range(3)]
        for d in range(3):
            older[d] = y[d]
        for d in STRAIGHT:
            cps[8 * k + d].wait_recv()
        for m, v in enumerate(combined(lambda m, k=k: drecv[k, m], False)):
            qdb[BLOCKS + m] = ghost_rows(v)

        def corner_next(k=k):
            for d in DIAGONAL:
                cps[8 * k + d].wait_recv()
            [v] = combined(lambda m: drecv[k, m], True)
            return ghost_rows(v)

        rate = rates_of(y, eta, corner_next)
        y = [base[d] + mut * dt * rate[d] for d in range(3)]

    for d in range(3):
        bfl_o[16 * d : 16 * (d + 1), :] = y[d]
    for c in pay_copies + cps:
        c.wait_send()


def finish(rho_p, mom_p, bfl_p, psi_p, rho_h, mom_h, bfl_h, psi_h, mom_r, bfl_r, sems):
    first = [
        pltpu.make_async_copy(rho_p, rho_h, sems.at[0]),
        pltpu.make_async_copy(psi_p, psi_h, sems.at[1]),
    ]
    for c in first:
        c.start()
    for src, dst in ((mom_p, mom_r), (bfl_p, bfl_r)):
        for j in range(BLOCKS):
            dst[:, TILE * j : TILE * (j + 1)] = src[pl.ds(j, 3, stride=16), :]
    second = [
        pltpu.make_async_copy(mom_r, mom_h, sems.at[2]),
        pltpu.make_async_copy(bfl_r, bfl_h, sems.at[3]),
    ]
    for c in second:
        c.start()
    for c in first + second:
        c.wait()


def shards(
    positions, density, momentum, field, psi, ohmic, ambipolar, ghost_index, tile_i, tile_j, tile_count
):
    def pin(v):
        return pltpu.with_memory_space_constraint(v, pltpu.HBM) if v.shape[0] != 1 else v

    def two(v):
        return v.reshape(BLOCKS, TILE)

    vmem = pl.BlockSpec(memory_space=pltpu.VMEM)
    hbm = pl.BlockSpec(memory_space=pltpu.HBM)
    V = pltpu.VMEM
    I32 = jnp.int32
    D = pltpu.SemaphoreType.DMA
    out = pl.pallas_call(
        kernel,
        out_shape=(
            jax.ShapeDtypeStruct((BLOCKS, TILE), F32),
            jax.ShapeDtypeStruct((48, TILE), F32),
            jax.ShapeDtypeStruct((48, TILE), F32),
            jax.ShapeDtypeStruct((BLOCKS, TILE), F32),
        ),
        in_specs=[hbm] * 11,
        out_specs=(vmem,) * 4,
        scratch_shapes=[
            V((3, 2048), F32), V((16, TILE), F32), V((3, 2048), F32), V((3, 2048), F32),
            V((16, TILE), F32), V((16, TILE), F32), V((16, TILE), F32),
            V((1024,), I32), pltpu.SMEM((64,), I32), pltpu.SMEM((64,), I32), pltpu.SMEM((64,), I32), pltpu.SMEM((1,), I32),
            V((8, TILE), I32), pltpu.SMEM((8, TILE), I32),
            V((144, TILE), F32),
            V((GBLOCKS, 8, TILE), jnp.int32),
            V((GBLOCKS, 8, TILE), jnp.int32),
            V((256, TILE), F32),
            V((NPIECE, 16, TILE), F32),
            V((NPIECE, 16, TILE), F32),
            V((256, TILE), F32),
            V((QROWS, BLOCKS, TILE), F32),
            V((32 * QROWS, TILE), F32),
            V((25, 2 * QROWS, TILE), BF16),
            V((25, 8, TILE), F32),
            V((25, 3, TILE, TILE), F32),
            V((TILES + 1, 2 * TILE, TILE), BF16),
            V((BLOCKS, 2 * TILE, TILE), BF16),
            V((TILES + 1, QROWS, TILE), F32),
            V((BLOCKS * QROWS, TILE), F32),
            V((64, TILE), F32),
            V((BLOCKS * 8, TILE), F32),
            V((SECTIONS, NPIECE, 8, TILE), F32),
            V((SECTIONS, NPIECE, 8, TILE), F32),
            V((25, 16, TILE), BF16),
            V((TILES + 1, 8, TILE), F32),
            V((BLOCKS * 8, TILE), F32),
            V((3, BLOCKS, TILE), F32),
            V((3, BLOCKS, TILE), F32),
            V((3, BLOCKS, TILE), F32),
            V((3, BLOCKS, TILE), F32),
            V((BLOCKS, TILE), F32),
            V((3, 1, TILE), F32),
            V((16, 1, TILE), F32),
            V((8, 1, TILE), F32),
            V((4, 1, TILE), F32),
            D((12,)), D, D((8,)), D((8,)), D((SECTIONS, 8)), D((SECTIONS, 8)),
            D((16,)), D((16,)), D((8,)), D((8,)), D((4,)), D((4,)),
        ],
        compiler_params=pltpu.CompilerParams(
            collective_id=0, has_side_effects=True, vmem_limit_bytes=48 * 1024 * 1024
        ),
    )(*map(pin, [
        positions, two(density), momentum, field, two(psi), two(ohmic), two(ambipolar),
        ghost_index, tile_i, tile_j, tile_count,
    ]))
    out = pl.pallas_call(
        finish,
        out_shape=(
            jax.ShapeDtypeStruct((BLOCKS, TILE), F32),
            jax.ShapeDtypeStruct((3, 2048), F32),
            jax.ShapeDtypeStruct((3, 2048), F32),
            jax.ShapeDtypeStruct((BLOCKS, TILE), F32),
        ),
        in_specs=[vmem] * 4,
        out_specs=(hbm,) * 4,
        scratch_shapes=[V((3, 2048), F32), V((3, 2048), F32), D((4,))],
        compiler_params=pltpu.CompilerParams(vmem_limit_bytes=1024 * 1024),
    )(*out)
    return out[0].reshape(-1), out[1], out[2], out[3].reshape(-1)


def solution(mesh):
    one, three = P(("gx", "gy")), P(None, ("gx", "gy"))
    return jax.shard_map(
        shards,
        mesh=mesh,
        in_specs=(three, one, three, three, one, one, one, one, one, one, one),
        out_specs=(one, three, three, one),
        check_vma=False,
    )
```
